256 devices in a mesh: context: 16 (over z_lo, x), tensor: 16 (over z_hi, y, core).
Axes of the slice: x: 4, y: 4, z: 8 (z_hi: 2, z_lo: 4; z = z_hi * 4 + z_lo), core: 2. Of those that a mesh axis runs over, the one named last changes fastest.
Arguments:
- tokens: bfloat16 [32768, 4096], P(('context', 'tensor')), may hold values from -6 to 6
- norm_gain: bfloat16 [4096], replicated, may hold values from 0.5 to 1.5
- in_weight: bfloat16 [4096, 3, 4096], P(None, None, 'tensor'), may hold values from -0.09375 to 0.09375
- short_filter: bfloat16 [3, 3, 4096], P(None, None, 'tensor'), may hold values from -3.5 to 3.5
- long_filter: bfloat16 [256, 128], P('tensor'), may hold values from -0.5 to 0.5
- doc_start: int32 [32768], P('context'), may hold values from 0 to 32767, as said below
Outputs:
- layer_out: bfloat16 [32768, 4096], P(('context', 'tensor'))
The draws below stay inside these ranges and needn't reach their ends.
Inputs may be any that keep to these rules, and one draw needn't show every extreme that they name: doc_start[0] = 0, and for t > 0 doc_start[t] is either doc_start[t - 1] or t, so documents are contiguous runs of positions; the last position begins a document.
All inputs are finite; a program needn't handle non-finite values.
Results may differ from the reference program's by a relative error of at most 0.0089.
Values may be sent and summed in bfloat16 or wider, within the bound.
No kernel may reach another device: no remote copies, remote signals or barrier semaphores. Data moves between devices by JAX's collectives and lax.ppermute only.
A program may use at most 128 MiB of HBM per device.

```python
import jax
import jax.numpy as jnp
from jax import lax

D = 4096
TAPS = 128
SHORT = 3
GROUP = 16
TOK_CTX = 2048
TOKENS = 32768
FILTERS = 256


def draw_doc_start(key, part):
    key = jax.random.fold_in(key, 11)
    marks = jax.random.randint(key, (TOKENS,), 0, TOK_CTX) < 2
    places = jnp.arange(TOKENS, dtype=jnp.int32)
    marks = jnp.where(places == 0, True, marks)
    marks = jnp.where(places == TOKENS - 1, True, marks)
    return lax.cummax(jnp.where(marks, places, 0), axis=0).astype(jnp.int32)


def level_of(rng, dims, cuts, smallest, largest):
    factor_of, own = 1.0, jax.random.fold_in(rng, 6)
    for dim, blocks in cuts:
        heights = jnp.exp(jax.random.uniform(jax.random.fold_in(own, dim), (blocks,), jnp.float32, smallest / len(cuts), largest / len(cuts)))
        factor_of = factor_of * jnp.repeat(heights, dims[dim] // blocks).reshape([-1 if axis == dim else 1 for axis in range(len(dims))])
    return factor_of


def centred(rng, extent, deviation, bound, cuts=(), kind=jnp.bfloat16):
    drawn = deviation * jax.random.normal(rng, extent, jnp.float32)
    if cuts:
        drawn = drawn * level_of(rng, extent, cuts, -0.22, 0.18)
    return jnp.clip(drawn, -bound, bound).astype(kind)


def setup_inputs(seed: int = 0) -> dict:
    seeds = jax.random.split(jax.random.key(seed), 7)
    return {
        "tokens": centred(seeds[0], (TOKENS, D), 1.0, 6.0, ((0, 256),)),
        "norm_gain": jnp.clip(1.0 + 0.1 * jax.random.normal(seeds[1], (D,), jnp.float32), 0.5, 1.5).astype(jnp.bfloat16),
        "in_weight": centred(seeds[2], (D, 3, D), D ** -0.5, 0.09375, ((2, 16),)),
        "short_filter": centred(seeds[3], (3, SHORT, D), SHORT ** -0.5, 3.5, ((2, 16),)),
        "long_filter": centred(seeds[4], (FILTERS, TAPS), TAPS ** -0.5, 0.5, ((0, 16),)),
        "doc_start": draw_doc_start(jax.random.fold_in(seeds[6], 71), 0),
    }


def banded(long_filter, span):
    groups = long_filter.shape[0]
    reversed_pad = jnp.concatenate([long_filter[:, ::-1], jnp.zeros((groups, span), long_filter.dtype)], axis=1)
    tiled = jnp.tile(reversed_pad, (1, span))[:, :span * (2 * span - 1)]
    return tiled.reshape(groups, span, 2 * span - 1)

def reference(tokens, norm_gain, in_weight, short_filter, long_filter, doc_start):
    float_tokens = tokens.astype(jnp.float32)
    scale_rows = lax.rsqrt(lax.optimization_barrier(jnp.mean(float_tokens * float_tokens, axis=-1, keepdims=True)) + 1e-06)
    normed = (float_tokens * scale_rows * norm_gain.astype(jnp.float32)[None]).astype(jnp.bfloat16)
    projected = jnp.dot(normed, in_weight.reshape(D, 3 * D), preferred_element_type=jnp.float32)
    projected = projected.astype(jnp.bfloat16).reshape(TOKENS, 3, D)
    places = jnp.arange(TOKENS, dtype=jnp.int32)
    mixed = jnp.zeros((TOKENS, 3, D), jnp.float32)
    for lag_step in range(SHORT):
        rolled = jnp.roll(projected, lag_step, axis=0).astype(jnp.float32)
        kept_mask = (places - lag_step >= doc_start)[:, None, None]
        mixed = mixed + jnp.where(kept_mask, short_filter[:, lag_step, :].astype(jnp.float32)[None] * rolled, 0.0)
    key_value = (mixed[:, 1] * mixed[:, 2]).astype(jnp.bfloat16)
    toeplitz = banded(long_filter, TAPS).astype(jnp.float32)
    extended = jnp.concatenate([jnp.zeros((TAPS - 1, D), jnp.bfloat16), key_value], axis=0)

    def one_block(block_index):
        first = (block_index * TAPS).astype(jnp.int32)
        window = lax.dynamic_slice_in_dim(extended, first, 2 * TAPS - 1, 0).astype(jnp.float32)
        window = window.reshape(2 * TAPS - 1, FILTERS, GROUP)
        block_starts = lax.dynamic_slice_in_dim(doc_start, first, TAPS, 0)
        inputs = first + jnp.arange(2 * TAPS - 1, dtype=jnp.int32) - (TAPS - 1)
        kept_mask = inputs[None, :] >= block_starts[:, None]
        weights = jnp.where(kept_mask[None], toeplitz, 0.0)
        return jnp.einsum('gij,jgc->igc', weights, window).reshape(TAPS, D)
    conv = lax.map(one_block, jnp.arange(TOKENS // TAPS, dtype=jnp.int32)).reshape(TOKENS, D)
    gated = (mixed[:, 0] * conv).astype(jnp.bfloat16)
    return (float_tokens + gated.astype(jnp.float32)).astype(jnp.bfloat16)
```

```python
import functools

import jax
import jax.numpy as jnp
from jax import lax
from jax.experimental import pallas as pl
from jax.experimental.pallas import tpu as pltpu
from jax.sharding import Mesh
from jax.sharding import PartitionSpec as P

AXES = ("z_lo", "x", "z_hi", "y", "core")
SPAN = 128
RIM = 16


def swap(value, axis):
    return lax.ppermute(value, axis, [(0, 1), (1, 0)])


def banded(long_filter):
    groups, span = long_filter.shape
    period = 3 * span
    row = jnp.concatenate([long_filter, jnp.zeros((groups, period - span), long_filter.dtype)], axis=1)
    tiled = jnp.tile(row, (1, 2 * span))[:, : 2 * span * (period - 1)]
    skewed = tiled.reshape(groups, 2 * span, period - 1)
    return skewed[:, :, span : 2 * span]


def gather_tokens(normed):
    rows, width = normed.shape
    y, core = lax.axis_index("y"), lax.axis_index("core")
    size = lax.axis_size("y")
    sib = swap(normed, "core")
    first = jnp.where(core == 0, normed, sib)
    second = jnp.where(core == 0, sib, normed)
    pair = jnp.concatenate([first, second], axis=0)
    ring = [
        (2 * i + c, 2 * ((i + (1 if c == 0 else -1)) % size) + c) for i in range(size) for c in range(2)
    ]
    near = lax.ppermute(pair, ("y", "core"), ring)
    near_half = lax.dynamic_slice_in_dim(near, core * rows, rows, 0)
    far = lax.ppermute(near_half, ("y", "core"), ring)
    near_sib = swap(near, "core")
    far_sib = swap(far, "core")
    sign = 1 - 2 * core
    full = jnp.zeros((2 * size * rows, width), normed.dtype)
    put = lambda full, value, at: lax.dynamic_update_slice_in_dim(full, value, at * rows, 0)
    full = put(full, pair, 2 * y)
    full = put(full, near, 2 * ((y - sign + size) % size))
    full = put(full, near_sib, 2 * ((y + sign + size) % size))
    full = put(full, far, 2 * ((y + 2) % size) + core)
    full = put(full, far_sib, 2 * ((y + 2) % size) + 1 - core)
    return full


def mix_conv_kernel(
    flags, proj, halo, short, band, start_col, start_row, out, key_value_t, query, conv_t
):
    length, channels = out.shape
    groups = band.shape[0]
    share = channels // groups
    blocks = length // SPAN
    taps = short.shape[0] // 3
    key_value_t[:, 0:SPAN] = halo[0:SPAN, :].astype(jnp.float32).T.astype(jnp.bfloat16)
    for b in range(blocks):
        rows = slice(b * SPAN, (b + 1) * SPAN)
        starts = start_col[rows, :]
        places = b * SPAN + lax.broadcasted_iota(jnp.int32, (SPAN, 1), 0)
        mixed = []
        for m in range(3):
            cols = slice(m * channels, (m + 1) * channels)
            if b == 0:
                before = halo[SPAN + m * RIM : SPAN + (m + 1) * RIM, :]
            else:
                before = proj[b * SPAN - RIM : b * SPAN, cols]
            both = jnp.concatenate([before, proj[rows, cols]], axis=0).astype(jnp.float32)
            total = None
            for s in range(taps):
                term = short[m * taps + s : m * taps + s + 1, :] * both[RIM - s : RIM - s + SPAN]
                term = jnp.where(places - s >= starts, term, 0.0)
                total = term if total is None else total + term
            mixed.append(total)
        query[rows, :] = mixed[0]
        key_value_t[:, (b + 1) * SPAN : (b + 2) * SPAN] = (mixed[1] * mixed[2]).T.astype(jnp.bfloat16)
    for g in range(groups):
        rows = slice(g * share, (g + 1) * share)
        windows = jnp.concatenate(
            [key_value_t[rows, b * SPAN : (b + 2) * SPAN] for b in range(blocks)], axis=0
        )
        sums = jnp.dot(windows, band[g], preferred_element_type=jnp.float32)
        for b in range(blocks):
            conv_t[rows, b * SPAN : (b + 1) * SPAN] = sums[b * share : (b + 1) * share]
    for b in range(blocks):

        @pl.when(flags[b] > 0)
        def _(b=b):
            inputs = (b - 1) * SPAN + lax.broadcasted_iota(jnp.int32, (2 * SPAN, SPAN), 0)
            kept = (inputs >= start_row[:, b * SPAN : (b + 1) * SPAN])

            def one_group(g, _):
                rows = pl.ds(pl.multiple_of(g * share, share), share)
                weights = jnp.where(kept, band[g].astype(jnp.float32), 0.0).astype(jnp.bfloat16)
                conv_t[rows, b * SPAN : (b + 1) * SPAN] = jnp.dot(
                    key_value_t[rows, b * SPAN : (b + 2) * SPAN],
                    weights,
                    preferred_element_type=jnp.float32,
                )
                return 0

            lax.fori_loop(0, groups, one_group, 0, unroll=4)

    for b in range(blocks):
        rows = slice(b * SPAN, (b + 1) * SPAN)
        out[rows, :] = (query[rows, :] * conv_t[:, b * SPAN : (b + 1) * SPAN].T).astype(out.dtype)


def mix_conv(proj, halo, short, band, starts):
    length = proj.shape[0]
    channels = proj.shape[1] // 3
    blocks = length // SPAN
    last = starts.reshape(blocks, SPAN)[:, -1]
    flags = (last > jnp.arange(blocks, dtype=jnp.int32) * SPAN - (SPAN - 1)).astype(jnp.int32)
    vmem = pl.BlockSpec(memory_space=pltpu.VMEM)
    return pl.pallas_call(
        mix_conv_kernel,
        out_shape=jax.ShapeDtypeStruct((length, channels), jnp.bfloat16),
        in_specs=[pl.BlockSpec(memory_space=pltpu.SMEM)] + [vmem] * 6,
        out_specs=vmem,
        scratch_shapes=[
            pltpu.VMEM((channels, length + SPAN), jnp.bfloat16),
            pltpu.VMEM((length, channels), jnp.float32),
            pltpu.VMEM((channels, length), jnp.float32),
        ],
        compiler_params=pltpu.CompilerParams(vmem_limit_bytes=24 << 20),
        cost_estimate=pl.CostEstimate(flops=10_000_000_000, bytes_accessed=4_000_000, transcendentals=0),
    )(flags, proj, halo, short, band, starts[:, None], starts[None, :])


def tail_of(proj, short, starts):
    length = proj.shape[0]
    channels = proj.shape[1] // 3
    taps = short.shape[0] // 3
    places = jnp.arange(length - SPAN, length, dtype=jnp.int32)
    mixed = []
    for m in (1, 2):
        total = jnp.zeros((SPAN, channels), jnp.float32)
        for s in range(taps):
            rows = proj[length - SPAN - s : length - s, m * channels : (m + 1) * channels].astype(jnp.float32)
            kept = (places - s >= starts[length - SPAN :])[:, None]
            total = total + jnp.where(kept, short[m * taps + s][None] * rows, 0.0)
        mixed.append(total)
    key_value = (mixed[0] * mixed[1]).astype(jnp.bfloat16)
    rims = [proj[length - RIM :, m * channels : (m + 1) * channels] for m in range(3)]
    return jnp.concatenate([key_value, *rims], axis=0)


def per_device(tokens, norm_gain, in_weight, short_filter, long_filter, doc_start):
    rows, width = tokens.shape
    channels = in_weight.shape[2]
    groups, span = long_filter.shape
    taps = short_filter.shape[1]
    z_lo, x, z_hi = lax.axis_index("z_lo"), lax.axis_index("x"), lax.axis_index("z_hi")
    contexts = lax.axis_size("z_lo") * lax.axis_size("x")
    context = z_lo * lax.axis_size("x") + x
    length = rows * lax.axis_size("y") * lax.axis_size("core")
    starts = lax.dynamic_slice_in_dim(doc_start, z_hi * length, length, 0)
    starts = starts - (context * lax.axis_size("z_hi") + z_hi) * length

    deep = width // contexts
    piece = lax.dynamic_slice_in_dim(in_weight, context * deep, deep, 0).reshape(deep, 3 * channels)
    piece = swap(piece, "z_hi")
    other_weight = lax.all_gather(piece, ("z_lo", "x"), axis=0, tiled=True)

    float_tokens = tokens.astype(jnp.float32)
    scale_rows = lax.rsqrt(jnp.mean(float_tokens * float_tokens, axis=-1, keepdims=True) + 1e-06)
    normed = (float_tokens * scale_rows * norm_gain.astype(jnp.float32)[None]).astype(jnp.bfloat16)
    gathered = gather_tokens(normed)

    small = jnp.concatenate(
        [short_filter.reshape(3 * taps, channels), long_filter.reshape(-1, channels)], axis=0
    )
    small = swap(small, "z_hi")
    other_short, other_long = small[: 3 * taps], small[3 * taps :].reshape(groups, span)

    next_half = [(i, i + 1) for i in range(contexts * lax.axis_size("z_hi") - 1)]

    def project(weight, short):
        projected = jnp.dot(gathered, weight, preferred_element_type=jnp.float32).astype(jnp.bfloat16)
        return projected, lax.ppermute(tail_of(projected, short, starts), ("z_lo", "x", "z_hi"), next_half)

    def finish(projected, halo, short, long):
        gated = mix_conv(projected, halo, short, banded(long), starts)
        return lax.all_to_all(gated, ("y", "core"), split_axis=0, concat_axis=1, tiled=True)

    own_short = short_filter.reshape(3 * taps, channels).astype(jnp.float32)
    other_short = other_short.astype(jnp.float32)
    own_projected, other_halo = project(in_weight.reshape(width, 3 * channels), own_short)
    other_projected, own_halo = project(other_weight, other_short)
    own = finish(own_projected, own_halo, own_short, long_filter)
    other = finish(other_projected, other_halo, other_short, other_long)
    left = jnp.where(z_hi == 0, own, other)
    right = jnp.where(z_hi == 0, other, own)
    gated = jnp.concatenate([left, right], axis=1)
    return (float_tokens + gated.astype(jnp.float32)).astype(jnp.bfloat16)


def solution(mesh):
    fine = Mesh(mesh.devices.reshape(4, 4, 2, 4, 2), AXES)
    context, tensor = ("z_lo", "x"), ("z_hi", "y", "core")
    in_specs = (
        P(context + tensor, None),
        P(),
        P(None, None, tensor),
        P(None, None, tensor),
        P(tensor, None),
        P(context),
    )
    return jax.shard_map(
        per_device, mesh=fine, in_specs=in_specs, out_specs=P(context + tensor, None), check_vma=False
    )
```

```python
import functools

import jax
import jax.numpy as jnp
from jax import lax
from jax.experimental import pallas as pl
from jax.experimental.pallas import tpu as pltpu
from jax.sharding import Mesh
from jax.sharding import PartitionSpec as P

AXES = ("z_lo", "x", "z_hi", "y", "core")
SPAN = 128
RIM = 16


def swap(value, axis):
    return lax.ppermute(value, axis, [(0, 1), (1, 0)])


def shift(value, axis, by):
    size = lax.axis_size(axis)
    return lax.ppermute(value, axis, [(i, (i + by) % size) for i in range(size)])


def fan(axis):
    size = lax.axis_size(axis)
    return [(2 * i + c, 2 * ((i + 1 - 2 * c) % size) + c) for i in range(size) for c in range(2)]


def band_kernel(taps, band):
    groups, span = taps.shape
    for g in range(groups):
        row = jnp.concatenate([taps[g : g + 1, :], jnp.zeros((1, span), jnp.float32)], axis=1)
        rows = jnp.broadcast_to(row, (2 * span, 2 * span))
        moved = pltpu.roll(rows, 0, axis=1, stride=1, stride_axis=0)
        band[g] = moved[:, span:].astype(band.dtype)


def banded(long_filter):
    groups, span = long_filter.shape
    vmem = pl.BlockSpec(memory_space=pltpu.VMEM)
    return pl.pallas_call(
        band_kernel,
        out_shape=jax.ShapeDtypeStruct((groups, 2 * span, span), jnp.bfloat16),
        in_specs=[vmem],
        out_specs=vmem,
        compiler_params=pltpu.CompilerParams(vmem_limit_bytes=16 << 20),
        cost_estimate=pl.CostEstimate(flops=2_000_000_000, bytes_accessed=1_000_000, transcendentals=0),
    )(long_filter.astype(jnp.float32))


def place(pieces, at, rows):
    width = pieces[0].shape[1]
    counts = [piece.shape[0] // rows for piece in pieces]
    firsts = [sum(counts[:n]) for n in range(len(pieces))]

    def kernel(at, *refs):
        del at
        step = pl.program_id(0)
        for n, (first, count) in enumerate(zip(firsts, counts)):

            @pl.when(jnp.logical_and(step >= first, step < first + count))
            def _(n=n):
                refs[-1][...] = refs[n][...]

    def pick(first, count):
        return pl.BlockSpec((rows, width), lambda step, at: (jnp.clip(step - first, 0, count - 1), 0))

    spec = pltpu.PrefetchScalarGridSpec(
        num_scalar_prefetch=1,
        grid=(sum(counts),),
        in_specs=[pick(first, count) for first, count in zip(firsts, counts)],
        out_specs=pl.BlockSpec((rows, width), lambda step, at: (at[step], 0)),
    )
    return pl.pallas_call(
        kernel,
        out_shape=jax.ShapeDtypeStruct((sum(counts) * rows, width), pieces[0].dtype),
        grid_spec=spec,
        compiler_params=pltpu.CompilerParams(vmem_limit_bytes=24 << 20),
        cost_estimate=pl.CostEstimate(flops=0, bytes_accessed=16_000_000, transcendentals=0),
    )(jnp.stack(at).astype(jnp.int32), *pieces)


def gather_tokens(normed):
    rows = normed.shape[0]
    y, core = lax.axis_index("y"), lax.axis_index("core")
    size = lax.axis_size("y")
    sib = swap(normed, "core")
    pair = jnp.concatenate([jnp.where(core == 0, normed, sib), jnp.where(core == 0, sib, normed)], axis=0)
    near = lax.ppermute(pair, ("y", "core"), fan("y"))
    near_half = lax.dynamic_slice_in_dim(near, core * rows, rows, 0)
    far = lax.ppermute(near_half, ("y", "core"), fan("y"))
    near_sib = swap(near, "core")
    far_sib = swap(far, "core")
    sign = 1 - 2 * core
    at = [2 * a + c for a in (y, (y - sign + size) % size, (y + sign + size) % size) for c in range(2)]
    at += [2 * ((y + 2) % size) + core, 2 * ((y + 2) % size) + 1 - core]
    return place([pair, near, near_sib, far, far_sib], at, rows)


def spread_columns(piece):
    up, down = shift(piece, "z_lo", 1), shift(piece, "z_lo", -1)
    late, up, down = lax.optimization_barrier((piece, up, down))
    return (0, piece), (1, up), (-1, down), (2, shift(late, "z_lo", 2))


def spread_rows(by, mine):
    z_lo, x, core = lax.axis_index("z_lo"), lax.axis_index("x"), lax.axis_index("core")
    depth, size = lax.axis_size("z_lo"), lax.axis_size("x")
    below, above = shift(mine, "x", 1), shift(mine, "x", -1)
    far = lax.ppermute(jnp.where(core == 0, below, above), ("x", "core"), fan("x"))
    first = (z_lo - by + depth) % depth * size
    places = [first + x, first + (x + size - 1) % size, first + (x + 1) % size, first + (x + 2) % size]
    return [mine, below, above, far], places


def add_product_kernel(count, places, *refs):
    del places
    lefts, rights, rest = refs[:count], refs[count : 2 * count], refs[2 * count :]
    total = rest[0][...] if len(rest) == 2 else None
    for left, right in zip(lefts, rights):
        term = jnp.dot(left[...], right[...], preferred_element_type=jnp.float32)
        total = term if total is None else total + term
    rest[-1][...] = total.astype(rest[-1].dtype)


def add_product(left, pieces, places, total, dtype):
    length = left.shape[0]
    deep, wide = pieces[0].shape
    rows = 256
    count = len(pieces)
    spec = pltpu.PrefetchScalarGridSpec(
        num_scalar_prefetch=1,
        grid=(length // rows,),
        in_specs=[pl.BlockSpec((rows, deep), lambda r, at, n=n: (r, at[n])) for n in range(count)]
        + [pl.BlockSpec((deep, wide), lambda r, at: (0, 0)) for _ in range(count)]
        + ([] if total is None else [pl.BlockSpec((rows, wide), lambda r, at: (r, 0))]),
        out_specs=pl.BlockSpec((rows, wide), lambda r, at: (r, 0)),
    )
    return pl.pallas_call(
        functools.partial(add_product_kernel, count),
        out_shape=jax.ShapeDtypeStruct((length, wide), dtype),
        grid_spec=spec,
        compiler_params=pltpu.CompilerParams(vmem_limit_bytes=24 << 20),
        cost_estimate=pl.CostEstimate(
            flops=2 * length * deep * wide * count, bytes_accessed=8_000_000, transcendentals=0
        ),
    )(jnp.stack(places).astype(jnp.int32), *[left] * count, *pieces, *([] if total is None else [total]))


def mix_conv_kernel(
    flags, proj, halo, short, band, start_col, start_row, out, key_value_t, query, conv_t
):
    length, channels = out.shape
    groups = band.shape[0]
    share = channels // groups
    blocks = length // SPAN
    taps = short.shape[0] // 3
    key_value_t[:, 0:SPAN] = halo[0:SPAN, :].astype(jnp.float32).T.astype(jnp.bfloat16)
    for b in range(blocks):
        rows = slice(b * SPAN, (b + 1) * SPAN)
        starts = start_col[rows, :]
        places = b * SPAN + lax.broadcasted_iota(jnp.int32, (SPAN, 1), 0)
        mixed = []
        for m in range(3):
            cols = slice(m * channels, (m + 1) * channels)
            if b == 0:
                before = halo[SPAN + m * RIM : SPAN + (m + 1) * RIM, :]
            else:
                before = proj[b * SPAN - RIM : b * SPAN, cols]
            both = jnp.concatenate([before, proj[rows, cols]], axis=0).astype(jnp.float32)
            total = None
            for s in range(taps):
                term = short[m * taps + s : m * taps + s + 1, :] * both[RIM - s : RIM - s + SPAN]
                term = jnp.where(places - s >= starts, term, 0.0)
                total = term if total is None else total + term
            mixed.append(total)
        query[rows, :] = mixed[0]
        key_value_t[:, (b + 1) * SPAN : (b + 2) * SPAN] = (mixed[1] * mixed[2]).T.astype(jnp.bfloat16)
    for g in range(groups):
        rows = slice(g * share, (g + 1) * share)
        windows = jnp.concatenate(
            [key_value_t[rows, b * SPAN : (b + 2) * SPAN] for b in range(blocks)], axis=0
        )
        sums = jnp.dot(windows, band[g], preferred_element_type=jnp.float32)
        for b in range(blocks):
            conv_t[rows, b * SPAN : (b + 1) * SPAN] = sums[b * share : (b + 1) * share]
    for b in range(blocks):

        @pl.when(flags[b] > 0)
        def _(b=b):
            inputs = (b - 1) * SPAN + lax.broadcasted_iota(jnp.int32, (2 * SPAN, SPAN), 0)
            kept = (inputs >= start_row[:, b * SPAN : (b + 1) * SPAN])

            def one_group(g, _):
                rows = pl.ds(pl.multiple_of(g * share, share), share)
                weights = jnp.where(kept, band[g].astype(jnp.float32), 0.0).astype(jnp.bfloat16)
                conv_t[rows, b * SPAN : (b + 1) * SPAN] = jnp.dot(
                    key_value_t[rows, b * SPAN : (b + 2) * SPAN],
                    weights,
                    preferred_element_type=jnp.float32,
                )
                return 0

            lax.fori_loop(0, groups, one_group, 0, unroll=4)

    for b in range(blocks):
        rows = slice(b * SPAN, (b + 1) * SPAN)
        out[rows, :] = (query[rows, :] * conv_t[:, b * SPAN : (b + 1) * SPAN].T).astype(out.dtype)


def mix_conv(proj, halo, short, band, starts):
    length = proj.shape[0]
    channels = proj.shape[1] // 3
    blocks = length // SPAN
    last = starts.reshape(blocks, SPAN)[:, -1]
    flags = (last > jnp.arange(blocks, dtype=jnp.int32) * SPAN - (SPAN - 1)).astype(jnp.int32)
    vmem = pl.BlockSpec(memory_space=pltpu.VMEM)
    return pl.pallas_call(
        mix_conv_kernel,
        out_shape=jax.ShapeDtypeStruct((length, channels), jnp.bfloat16),
        in_specs=[pl.BlockSpec(memory_space=pltpu.SMEM)] + [vmem] * 6,
        out_specs=vmem,
        scratch_shapes=[
            pltpu.VMEM((channels, length + SPAN), jnp.bfloat16),
            pltpu.VMEM((length, channels), jnp.float32),
            pltpu.VMEM((channels, length), jnp.float32),
        ],
        compiler_params=pltpu.CompilerParams(vmem_limit_bytes=24 << 20),
        cost_estimate=pl.CostEstimate(flops=10_000_000_000, bytes_accessed=4_000_000, transcendentals=0),
    )(flags, proj, halo, short, band, starts[:, None], starts[None, :])


def tail_of(proj, short, starts):
    length = proj.shape[0]
    channels = proj.shape[1] // 3
    taps = short.shape[0] // 3
    places = jnp.arange(length - SPAN, length, dtype=jnp.int32)
    mixed = []
    for m in (1, 2):
        total = jnp.zeros((SPAN, channels), jnp.float32)
        for s in range(taps):
            rows = proj[length - SPAN - s : length - s, m * channels : (m + 1) * channels].astype(jnp.float32)
            kept = (places - s >= starts[length - SPAN :])[:, None]
            total = total + jnp.where(kept, short[m * taps + s][None] * rows, 0.0)
        mixed.append(total)
    key_value = (mixed[0] * mixed[1]).astype(jnp.bfloat16)
    rims = [proj[length - RIM :, m * channels : (m + 1) * channels] for m in range(3)]
    return jnp.concatenate([key_value, *rims], axis=0)


def per_device(tokens, norm_gain, in_weight, short_filter, long_filter, doc_start):
    rows, width = tokens.shape
    channels = in_weight.shape[2]
    groups, span = long_filter.shape
    taps = short_filter.shape[1]
    z_lo, x, z_hi = lax.axis_index("z_lo"), lax.axis_index("x"), lax.axis_index("z_hi")
    contexts = lax.axis_size("z_lo") * lax.axis_size("x")
    context = z_lo * lax.axis_size("x") + x
    length = rows * lax.axis_size("y") * lax.axis_size("core")
    starts = lax.dynamic_slice_in_dim(doc_start, z_hi * length, length, 0)
    starts = starts - (context * lax.axis_size("z_hi") + z_hi) * length

    deep = width // contexts
    piece = lax.dynamic_slice_in_dim(in_weight, context * deep, deep, 0).reshape(deep, 3 * channels)
    piece, tokens = lax.optimization_barrier((piece, tokens))
    piece = swap(piece, "z_hi")

    float_tokens = tokens.astype(jnp.float32)
    scale_rows = lax.rsqrt(jnp.mean(float_tokens * float_tokens, axis=-1, keepdims=True) + 1e-06)
    normed = (float_tokens * scale_rows * norm_gain.astype(jnp.float32)[None]).astype(jnp.bfloat16)
    in_weight, normed = lax.optimization_barrier((in_weight, normed))
    gathered = gather_tokens(normed)
    columns = spread_columns(piece)

    small = jnp.concatenate(
        [short_filter.reshape(3 * taps, channels), long_filter.reshape(-1, channels)], axis=0
    )
    small = swap(small, "z_hi")
    other_short, other_long = small[: 3 * taps], small[3 * taps :].reshape(groups, span)

    next_half = [(i, i + 1) for i in range(contexts * lax.axis_size("z_hi") - 1)]

    def halo_of(projected, short):
        return lax.ppermute(tail_of(projected, short, starts), ("z_lo", "x", "z_hi"), next_half)

    def finish(projected, halo, short, long):
        gated = mix_conv(projected, halo, short, banded(long), starts)
        return lax.all_to_all(gated, ("y", "core"), split_axis=0, concat_axis=1, tiled=True)

    own_short = short_filter.reshape(3 * taps, channels).astype(jnp.float32)
    other_short = other_short.astype(jnp.float32)
    own_projected = jnp.dot(
        gathered, in_weight.reshape(width, 3 * channels), preferred_element_type=jnp.float32
    ).astype(jnp.bfloat16)
    other_halo = halo_of(own_projected, own_short)
    other_projected = None
    for n, (by, mine) in enumerate(columns):
        last = n == len(columns) - 1
        if last:
            mine, own_projected = lax.optimization_barrier((mine, own_projected))
        pieces, places = spread_rows(by, mine)
        other_projected = add_product(
            gathered, pieces, places, other_projected, jnp.bfloat16 if last else jnp.float32
        )
    own_halo = halo_of(other_projected, other_short)
    own = finish(own_projected, own_halo, own_short, long_filter)
    other = finish(other_projected, other_halo, other_short, other_long)
    left = jnp.where(z_hi == 0, own, other)
    right = jnp.where(z_hi == 0, other, own)
    gated = jnp.concatenate([left, right], axis=1)
    return (float_tokens + gated.astype(jnp.float32)).astype(jnp.bfloat16)


def solution(mesh):
    fine = Mesh(mesh.devices.reshape(4, 4, 2, 4, 2), AXES)
    context, tensor = ("z_lo", "x"), ("z_hi", "y", "core")
    in_specs = (
        P(context + tensor, None),
        P(),
        P(None, None, tensor),
        P(None, None, tensor),
        P(tensor, None),
        P(context),
    )
    return jax.shard_map(
        per_device, mesh=fine, in_specs=in_specs, out_specs=P(context + tensor, None), check_vma=False
    )
```

```python
import functools

import jax
import jax.numpy as jnp
from jax import lax
from jax.experimental import pallas as pl
from jax.experimental.pallas import tpu as pltpu
from jax.sharding import Mesh
from jax.sharding import PartitionSpec as P

AXES = ("z_lo", "x", "z_hi", "y", "core")
SPAN = 128
RIM = 16


def swap(value, axis):
    return lax.ppermute(value, axis, [(0, 1), (1, 0)])


def shift(value, axis, by):
    size = lax.axis_size(axis)
    return lax.ppermute(value, axis, [(i, (i + by) % size) for i in range(size)])


def fan(axis):
    size = lax.axis_size(axis)
    return [(2 * i + c, 2 * ((i + 1 - 2 * c) % size) + c) for i in range(size) for c in range(2)]


def band_kernel(taps, band):
    groups, span = taps.shape
    for g in range(groups):
        row = jnp.concatenate([taps[g : g + 1, :], jnp.zeros((1, span), jnp.float32)], axis=1)
        rows = jnp.broadcast_to(row, (2 * span, 2 * span))
        moved = pltpu.roll(rows, 0, axis=1, stride=1, stride_axis=0)
        band[g] = moved[:, span:].astype(band.dtype)


def banded(long_filter):
    groups, span = long_filter.shape
    vmem = pl.BlockSpec(memory_space=pltpu.VMEM)
    return pl.pallas_call(
        band_kernel,
        out_shape=jax.ShapeDtypeStruct((groups, 2 * span, span), jnp.bfloat16),
        in_specs=[vmem],
        out_specs=vmem,
        compiler_params=pltpu.CompilerParams(vmem_limit_bytes=16 << 20),
        cost_estimate=pl.CostEstimate(flops=2_000_000_000, bytes_accessed=1_000_000, transcendentals=0),
    )(long_filter.astype(jnp.float32))


def spread_columns(piece):
    up, down = shift(piece, "z_lo", 1), shift(piece, "z_lo", -1)
    late, up, down = lax.optimization_barrier((piece, up, down))
    return (0, piece), (1, up), (-1, down), (2, shift(late, "z_lo", 2))


def spread_rows(mine):
    below, above = shift(mine, "x", 1), shift(mine, "x", -1)
    return below, above, jnp.where(lax.axis_index("core") == 0, below, above)


def places_of(by):
    z_lo, x = lax.axis_index("z_lo"), lax.axis_index("x")
    depth, size = lax.axis_size("z_lo"), lax.axis_size("x")
    first = (z_lo - by + depth) % depth * size
    return [first + x, first + (x + size - 1) % size, first + (x + 1) % size, first + (x + 2) % size]


def add_product_kernel(count, places, *refs):
    del places
    lefts, rights, rest = refs[:count], refs[count : 2 * count], refs[2 * count :]
    total = rest[0][...] if len(rest) == 2 else None
    for left, right in zip(lefts, rights):
        term = jnp.dot(left[...], right[...], preferred_element_type=jnp.float32)
        total = term if total is None else total + term
    rest[-1][...] = total.astype(rest[-1].dtype)


def add_product(left, pieces, places, total, dtype):
    length = left.shape[0]
    deep, wide = pieces[0].shape
    rows = 256
    count = len(pieces)
    spec = pltpu.PrefetchScalarGridSpec(
        num_scalar_prefetch=1,
        grid=(length // rows,),
        in_specs=[pl.BlockSpec((rows, deep), lambda r, at, n=n: (r, at[n])) for n in range(count)]
        + [pl.BlockSpec((deep, wide), lambda r, at: (0, 0)) for _ in range(count)]
        + ([] if total is None else [pl.BlockSpec((rows, wide), lambda r, at: (r, 0))]),
        out_specs=pl.BlockSpec((rows, wide), lambda r, at: (r, 0)),
    )
    return pl.pallas_call(
        functools.partial(add_product_kernel, count),
        out_shape=jax.ShapeDtypeStruct((length, wide), dtype),
        grid_spec=spec,
        compiler_params=pltpu.CompilerParams(vmem_limit_bytes=24 << 20),
        cost_estimate=pl.CostEstimate(
            flops=2 * length * deep * wide * count, bytes_accessed=8_000_000, transcendentals=0
        ),
    )(jnp.stack(places).astype(jnp.int32), *[left] * count, *pieces, *([] if total is None else [total]))


def mix_conv_kernel(
    flags, proj, halo, short, band, start_col, start_row, out, key_value_t, query, conv_t
):
    length, channels = out.shape
    groups = band.shape[0]
    share = channels // groups
    blocks = length // SPAN
    taps = short.shape[0] // 3
    key_value_t[:, 0:SPAN] = halo[0:SPAN, :].astype(jnp.float32).T.astype(jnp.bfloat16)
    for b in range(blocks):
        rows = slice(b * SPAN, (b + 1) * SPAN)
        starts = start_col[rows, :]
        places = b * SPAN + lax.broadcasted_iota(jnp.int32, (SPAN, 1), 0)
        mixed = []
        for m in range(3):
            cols = slice(m * channels, (m + 1) * channels)
            if b == 0:
                before = halo[SPAN + m * RIM : SPAN + (m + 1) * RIM, :]
            else:
                before = proj[b * SPAN - RIM : b * SPAN, cols]
            both = jnp.concatenate([before, proj[rows, cols]], axis=0).astype(jnp.float32)
            total = None
            for s in range(taps):
                term = short[m * taps + s : m * taps + s + 1, :] * both[RIM - s : RIM - s + SPAN]
                term = jnp.where(places - s >= starts, term, 0.0)
                total = term if total is None else total + term
            mixed.append(total)
        query[rows, :] = mixed[0]
        key_value_t[:, (b + 1) * SPAN : (b + 2) * SPAN] = (mixed[1] * mixed[2]).T.astype(jnp.bfloat16)
    for g in range(groups):
        rows = slice(g * share, (g + 1) * share)
        windows = jnp.concatenate(
            [key_value_t[rows, b * SPAN : (b + 2) * SPAN] for b in range(blocks)], axis=0
        )
        sums = jnp.dot(windows, band[g], preferred_element_type=jnp.float32)
        for b in range(blocks):
            conv_t[rows, b * SPAN : (b + 1) * SPAN] = sums[b * share : (b + 1) * share]
    for b in range(blocks):

        @pl.when(flags[b] > 0)
        def _(b=b):
            inputs = (b - 1) * SPAN + lax.broadcasted_iota(jnp.int32, (2 * SPAN, SPAN), 0)
            kept = (inputs >= start_row[:, b * SPAN : (b + 1) * SPAN])

            def one_group(g, _):
                rows = pl.ds(pl.multiple_of(g * share, share), share)
                weights = jnp.where(kept, band[g].astype(jnp.float32), 0.0).astype(jnp.bfloat16)
                conv_t[rows, b * SPAN : (b + 1) * SPAN] = jnp.dot(
                    key_value_t[rows, b * SPAN : (b + 2) * SPAN],
                    weights,
                    preferred_element_type=jnp.float32,
                )
                return 0

            lax.fori_loop(0, groups, one_group, 0, unroll=4)

    for b in range(blocks):
        rows = slice(b * SPAN, (b + 1) * SPAN)
        out[rows, :] = (query[rows, :] * conv_t[:, b * SPAN : (b + 1) * SPAN].T).astype(out.dtype)


def mix_conv(proj, halo, short, band, starts):
    length = proj.shape[0]
    channels = proj.shape[1] // 3
    blocks = length // SPAN
    last = starts.reshape(blocks, SPAN)[:, -1]
    flags = (last > jnp.arange(blocks, dtype=jnp.int32) * SPAN - (SPAN - 1)).astype(jnp.int32)
    vmem = pl.BlockSpec(memory_space=pltpu.VMEM)
    return pl.pallas_call(
        mix_conv_kernel,
        out_shape=jax.ShapeDtypeStruct((length, channels), jnp.bfloat16),
        in_specs=[pl.BlockSpec(memory_space=pltpu.SMEM)] + [vmem] * 6,
        out_specs=vmem,
        scratch_shapes=[
            pltpu.VMEM((channels, length + SPAN), jnp.bfloat16),
            pltpu.VMEM((length, channels), jnp.float32),
            pltpu.VMEM((channels, length), jnp.float32),
        ],
        compiler_params=pltpu.CompilerParams(vmem_limit_bytes=24 << 20),
        cost_estimate=pl.CostEstimate(flops=10_000_000_000, bytes_accessed=4_000_000, transcendentals=0),
    )(flags, proj, halo, short, band, starts[:, None], starts[None, :])


def tail_of(proj, short, starts):
    length = proj.shape[0]
    channels = proj.shape[1] // 3
    taps = short.shape[0] // 3
    places = jnp.arange(length - SPAN, length, dtype=jnp.int32)
    mixed = []
    for m in (1, 2):
        total = jnp.zeros((SPAN, channels), jnp.float32)
        for s in range(taps):
            rows = proj[length - SPAN - s : length - s, m * channels : (m + 1) * channels].astype(jnp.float32)
            kept = (places - s >= starts[length - SPAN :])[:, None]
            total = total + jnp.where(kept, short[m * taps + s][None] * rows, 0.0)
        mixed.append(total)
    key_value = (mixed[0] * mixed[1]).astype(jnp.bfloat16)
    rims = [proj[length - RIM :, m * channels : (m + 1) * channels] for m in range(3)]
    return jnp.concatenate([key_value, *rims], axis=0)


def per_device(tokens, norm_gain, in_weight, short_filter, long_filter, doc_start):
    rows, width = tokens.shape
    channels = in_weight.shape[2]
    groups, span = long_filter.shape
    taps = short_filter.shape[1]
    z_lo, x, z_hi = lax.axis_index("z_lo"), lax.axis_index("x"), lax.axis_index("z_hi")
    contexts = lax.axis_size("z_lo") * lax.axis_size("x")
    context = z_lo * lax.axis_size("x") + x
    length = rows * lax.axis_size("y") * lax.axis_size("core")
    starts = lax.dynamic_slice_in_dim(doc_start, z_hi * length, length, 0)
    starts = starts - (context * lax.axis_size("z_hi") + z_hi) * length

    deep = width // contexts
    piece = lax.dynamic_slice_in_dim(in_weight, context * deep, deep, 0).reshape(deep, 3 * channels)
    piece, tokens = lax.optimization_barrier((piece, tokens))
    piece = swap(piece, "z_hi")

    float_tokens = tokens.astype(jnp.float32)
    scale_rows = lax.rsqrt(jnp.mean(float_tokens * float_tokens, axis=-1, keepdims=True) + 1e-06)
    normed = (float_tokens * scale_rows * norm_gain.astype(jnp.float32)[None]).astype(jnp.bfloat16)
    in_weight, normed = lax.optimization_barrier((in_weight, normed))
    gathered = lax.all_gather(normed, ("y", "core"), axis=0, tiled=True)
    weight_t = in_weight.transpose(1, 2, 0).reshape(3 * channels, width)
    piece, weight_t = lax.optimization_barrier((piece, weight_t))
    columns = spread_columns(piece)

    small = jnp.concatenate(
        [short_filter.reshape(3 * taps, channels), long_filter.reshape(-1, channels)], axis=0
    )
    small = swap(small, "z_hi")
    other_short, other_long = small[: 3 * taps], small[3 * taps :].reshape(groups, span)

    next_half = [(i, i + 1) for i in range(contexts * lax.axis_size("z_hi") - 1)]

    def halo_of(projected, short):
        return lax.ppermute(tail_of(projected, short, starts), ("z_lo", "x", "z_hi"), next_half)

    def finish(projected, halo, short, long):
        gated = mix_conv(projected, halo, short, banded(long), starts)
        return lax.all_to_all(gated, ("y", "core"), split_axis=0, concat_axis=1, tiled=True)

    own_short = short_filter.reshape(3 * taps, channels).astype(jnp.float32)
    other_short = other_short.astype(jnp.float32)
    own_projected = lax.dot_general(
        gathered, weight_t, (((1,), (1,)), ((), ())), preferred_element_type=jnp.float32
    ).astype(jnp.bfloat16)
    rows_of = [spread_rows(mine) for _, mine in columns]
    other_projected = None
    for n, ((by, mine), (below, above, onward)) in enumerate(zip(columns, rows_of)):
        last = n == len(columns) - 1
        if n == len(columns) - 2:
            onward, own_projected = lax.optimization_barrier((onward, own_projected))
        far = lax.ppermute(onward, ("x", "core"), fan("x"))
        other_projected = add_product(
            gathered,
            [mine, below, above, far],
            places_of(by),
            other_projected,
            jnp.bfloat16 if last else jnp.float32,
        )
    other_halo = halo_of(own_projected, own_short)
    own_halo = halo_of(other_projected, other_short)
    own = finish(own_projected, own_halo, own_short, long_filter)
    other = finish(other_projected, other_halo, other_short, other_long)
    left = jnp.where(z_hi == 0, own, other)
    right = jnp.where(z_hi == 0, other, own)
    gated = jnp.concatenate([left, right], axis=1)
    return (float_tokens + gated.astype(jnp.float32)).astype(jnp.bfloat16)


def solution(mesh):
    fine = Mesh(mesh.devices.reshape(4, 4, 2, 4, 2), AXES)
    context, tensor = ("z_lo", "x"), ("z_hi", "y", "core")
    in_specs = (
        P(context + tensor, None),
        P(),
        P(None, None, tensor),
        P(None, None, tensor),
        P(tensor, None),
        P(context),
    )
    return jax.shard_map(
        per_device, mesh=fine, in_specs=in_specs, out_specs=P(context + tensor, None), check_vma=False
    )
```

```python
import functools

import jax
import jax.numpy as jnp
from jax import lax
from jax.experimental import pallas as pl
from jax.experimental.pallas import tpu as pltpu
from jax.sharding import Mesh
from jax.sharding import PartitionSpec as P

AXES = ("z_lo", "x", "z_hi", "y", "core")
SPAN = 128
RIM = 16


def swap(value, axis):
    return lax.ppermute(value, axis, [(0, 1), (1, 0)])


def shift(value, axis, by):
    size = lax.axis_size(axis)
    return lax.ppermute(value, axis, [(i, (i + by) % size) for i in range(size)])


def fan(axis):
    size = lax.axis_size(axis)
    return [(2 * i + c, 2 * ((i + 1 - 2 * c) % size) + c) for i in range(size) for c in range(2)]


def band_kernel(taps, band):
    groups, span = taps.shape
    for g in range(groups):
        row = jnp.concatenate([taps[g : g + 1, :], jnp.zeros((1, span), jnp.float32)], axis=1)
        rows = jnp.broadcast_to(row, (2 * span, 2 * span))
        moved = pltpu.roll(rows, 0, axis=1, stride=1, stride_axis=0)
        band[g] = moved[:, span:].astype(band.dtype)


def banded(long_filter):
    groups, span = long_filter.shape
    vmem = pl.BlockSpec(memory_space=pltpu.VMEM)
    return pl.pallas_call(
        band_kernel,
        out_shape=jax.ShapeDtypeStruct((groups, 2 * span, span), jnp.bfloat16),
        in_specs=[vmem],
        out_specs=vmem,
        compiler_params=pltpu.CompilerParams(vmem_limit_bytes=16 << 20),
        cost_estimate=pl.CostEstimate(flops=2_000_000_000, bytes_accessed=1_000_000, transcendentals=0),
    )(long_filter.astype(jnp.float32))


def across(value, by):
    size = lax.axis_size("z_lo")
    pairs = [(2 * i + h, 2 * ((i + by) % size) + 1 - h) for i in range(size) for h in range(2)]
    return lax.ppermute(value, ("z_lo", "z_hi"), pairs)


def ring(value, by):
    size = lax.axis_size("z_lo")
    pairs = []
    for i in range(size):
        for h in range(2):
            to = (h * size + i + by) % (2 * size)
            pairs.append((2 * i + h, 2 * (to % size) + to // size))
    return lax.ppermute(value, ("z_lo", "z_hi"), pairs)


def spread_columns(piece, ends):
    z_lo = lax.axis_index("z_lo")
    size = lax.axis_size("z_lo")
    top, bottom = z_lo == size - 1, z_lo == 0
    up = ring(jnp.where(top, ends[0], piece), 1)
    down = ring(jnp.where(bottom, ends[0], piece), -1)
    pairs = []
    for h in range(2):
        pairs += [(2 * 1 + h, 2 * 2 + h), (2 * 2 + h, 2 * 1 + h)]
        pairs += [(2 * 0 + h, 2 * 3 + 1 - h), (2 * 3 + h, 2 * 0 + 1 - h)]
    onward = jnp.where(jnp.logical_or(top, bottom), ends[1], jnp.where(z_lo == 1, up, down))
    opposite = lax.ppermute(onward, ("z_lo", "z_hi"), pairs)
    return (0, piece), (1, up), (-1, down), (2, opposite)


def spread_rows(mine):
    below, above = shift(mine, "x", 1), shift(mine, "x", -1)
    return below, above, jnp.where(lax.axis_index("core") == 0, below, above)


def places_of(by):
    z_lo, x = lax.axis_index("z_lo"), lax.axis_index("x")
    depth, size = lax.axis_size("z_lo"), lax.axis_size("x")
    first = (z_lo - by + depth) % depth * size
    return [first + x, first + (x + size - 1) % size, first + (x + 1) % size, first + (x + 2) % size]


def add_product_kernel(count, places, *refs):
    del places
    lefts, rights, rest = refs[:count], refs[count : 2 * count], refs[2 * count :]
    left = jnp.concatenate([ref[...] for ref in lefts], axis=1)
    right = jnp.concatenate([ref[...] for ref in rights], axis=0)
    total = jnp.dot(left, right, preferred_element_type=jnp.float32)
    if len(rest) == 2:
        total = total + rest[0][...]
    rest[-1][...] = total.astype(rest[-1].dtype)


def add_product(left, pieces, places, total, dtype):
    length = left.shape[0]
    deep, wide = pieces[0].shape
    rows = 512
    count = len(pieces)
    spec = pltpu.PrefetchScalarGridSpec(
        num_scalar_prefetch=1,
        grid=(length // rows,),
        in_specs=[pl.BlockSpec((rows, deep), lambda r, at, n=n: (r, at[n])) for n in range(count)]
        + [pl.BlockSpec((deep, wide), lambda r, at: (0, 0)) for _ in range(count)]
        + ([] if total is None else [pl.BlockSpec((rows, wide), lambda r, at: (r, 0))]),
        out_specs=pl.BlockSpec((rows, wide), lambda r, at: (r, 0)),
    )
    return pl.pallas_call(
        functools.partial(add_product_kernel, count),
        out_shape=jax.ShapeDtypeStruct((length, wide), dtype),
        grid_spec=spec,
        compiler_params=pltpu.CompilerParams(vmem_limit_bytes=40 << 20),
        cost_estimate=pl.CostEstimate(
            flops=2 * length * deep * wide * count, bytes_accessed=8_000_000, transcendentals=0
        ),
    )(jnp.stack(places).astype(jnp.int32), *[left] * count, *pieces, *([] if total is None else [total]))


def mix_conv_kernel(
    flags, proj, halo, short, band, start_col, start_row, into, out, key_value_t, query, conv_t
):
    del into
    length, channels = out.shape
    groups = band.shape[0]
    share = channels // groups
    blocks = length // SPAN
    taps = short.shape[0] // 3
    key_value_t[:, 0:SPAN] = halo[0:SPAN, :].astype(jnp.float32).T.astype(jnp.bfloat16)
    for b in range(blocks):
        rows = slice(b * SPAN, (b + 1) * SPAN)
        starts = start_col[rows, :]
        places = b * SPAN + lax.broadcasted_iota(jnp.int32, (SPAN, 1), 0)
        mixed = []
        for m in range(3):
            cols = slice(m * channels, (m + 1) * channels)
            if b == 0:
                before = halo[SPAN + m * RIM : SPAN + (m + 1) * RIM, :]
            else:
                before = proj[b * SPAN - RIM : b * SPAN, cols]
            both = jnp.concatenate([before, proj[rows, cols]], axis=0).astype(jnp.float32)
            total = None
            for s in range(taps):
                term = short[m * taps + s : m * taps + s + 1, :] * both[RIM - s : RIM - s + SPAN]
                term = jnp.where(places - s >= starts, term, 0.0)
                total = term if total is None else total + term
            mixed.append(total)
        query[rows, :] = mixed[0]
        key_value_t[:, (b + 1) * SPAN : (b + 2) * SPAN] = (mixed[1] * mixed[2]).T.astype(jnp.bfloat16)
    for g in range(groups):
        rows = slice(g * share, (g + 1) * share)
        windows = jnp.concatenate(
            [key_value_t[rows, b * SPAN : (b + 2) * SPAN] for b in range(blocks)], axis=0
        )
        sums = jnp.dot(windows, band[g], preferred_element_type=jnp.float32)
        for b in range(blocks):
            conv_t[rows, b * SPAN : (b + 1) * SPAN] = sums[b * share : (b + 1) * share]
    for b in range(blocks):

        @pl.when(flags[b] > 0)
        def _(b=b):
            inputs = (b - 1) * SPAN + lax.broadcasted_iota(jnp.int32, (2 * SPAN, SPAN), 0)
            kept = (inputs >= start_row[:, b * SPAN : (b + 1) * SPAN])

            def one_group(g, _):
                rows = pl.ds(pl.multiple_of(g * share, share), share)
                weights = jnp.where(kept, band[g].astype(jnp.float32), 0.0).astype(jnp.bfloat16)
                conv_t[rows, b * SPAN : (b + 1) * SPAN] = jnp.dot(
                    key_value_t[rows, b * SPAN : (b + 2) * SPAN],
                    weights,
                    preferred_element_type=jnp.float32,
                )
                return 0

            lax.fori_loop(0, groups, one_group, 0, unroll=4)

    for b in range(blocks):
        rows = slice(b * SPAN, (b + 1) * SPAN)
        out[rows, :] = (query[rows, :] * conv_t[:, b * SPAN : (b + 1) * SPAN].T).astype(out.dtype)


def mix_conv(proj, halo, short, band, starts, rows, into, side):
    length, channels = proj.shape[0], proj.shape[1] // 3
    blocks = rows // SPAN
    starts = starts[:rows]
    last = starts.reshape(blocks, SPAN)[:, -1]
    flags = (last > jnp.arange(blocks, dtype=jnp.int32) * SPAN - (SPAN - 1)).astype(jnp.int32)
    given = [flags, proj, halo, short, band, starts[:, None], starts[None, :]]
    in_specs = [pl.BlockSpec(memory_space=pltpu.SMEM), pl.BlockSpec((rows, 3 * channels), lambda n: (0, 0))]
    in_specs += [pl.BlockSpec(memory_space=pltpu.VMEM)] * 5
    body = mix_conv_kernel
    aliases = {}
    if into is None:
        body = lambda *refs: mix_conv_kernel(*refs[:7], None, *refs[7:])
    else:
        aliases = {len(given): 0}
        given.append(into)
        in_specs.append(pl.BlockSpec(memory_space=pl.ANY))
    return pl.pallas_call(
        body,
        out_shape=jax.ShapeDtypeStruct((length, 2 * channels), jnp.bfloat16),
        grid=(1,),
        in_specs=in_specs,
        out_specs=pl.BlockSpec((rows, channels), lambda n: (0, side)),
        scratch_shapes=[
            pltpu.VMEM((channels, rows + SPAN), jnp.bfloat16),
            pltpu.VMEM((rows, channels), jnp.float32),
            pltpu.VMEM((channels, rows), jnp.float32),
        ],
        input_output_aliases=aliases,
        compiler_params=pltpu.CompilerParams(vmem_limit_bytes=24 << 20),
        cost_estimate=pl.CostEstimate(flops=rows * 6_000_000, bytes_accessed=4_000_000, transcendentals=0),
    )(*given)


def tail_of(proj, short, starts):
    length = proj.shape[0]
    channels = proj.shape[1] // 3
    taps = short.shape[0] // 3
    places = jnp.arange(length - SPAN, length, dtype=jnp.int32)
    mixed = []
    for m in (1, 2):
        total = jnp.zeros((SPAN, channels), jnp.float32)
        for s in range(taps):
            rows = proj[length - SPAN - s : length - s, m * channels : (m + 1) * channels].astype(jnp.float32)
            kept = (places - s >= starts[length - SPAN :])[:, None]
            total = total + jnp.where(kept, short[m * taps + s][None] * rows, 0.0)
        mixed.append(total)
    key_value = (mixed[0] * mixed[1]).astype(jnp.bfloat16)
    rims = [proj[length - RIM :, m * channels : (m + 1) * channels] for m in range(3)]
    return jnp.concatenate([key_value, *rims], axis=0)


def per_device(tokens, norm_gain, in_weight, short_filter, long_filter, doc_start):
    rows, width = tokens.shape
    channels = in_weight.shape[2]
    groups, span = long_filter.shape
    taps = short_filter.shape[1]
    z_lo, x, z_hi = lax.axis_index("z_lo"), lax.axis_index("x"), lax.axis_index("z_hi")
    contexts = lax.axis_size("z_lo") * lax.axis_size("x")
    context = z_lo * lax.axis_size("x") + x
    length = rows * lax.axis_size("y") * lax.axis_size("core")
    starts = lax.dynamic_slice_in_dim(doc_start, z_hi * length, length, 0)
    starts = starts - (context * lax.axis_size("z_hi") + z_hi) * length

    deep = width // contexts
    depth = lax.axis_size("z_lo")

    def cut(quarter):
        first = (quarter * lax.axis_size("x") + x) * deep
        return lax.dynamic_slice_in_dim(in_weight, first, deep, 0).reshape(deep, 3 * channels)

    piece, tokens = lax.optimization_barrier((cut((z_lo + 2) % depth), tokens))
    piece = across(piece, 2)
    top = z_lo == depth - 1

    float_tokens = tokens.astype(jnp.float32)
    scale_rows = lax.rsqrt(jnp.mean(float_tokens * float_tokens, axis=-1, keepdims=True) + 1e-06)
    normed = (float_tokens * scale_rows * norm_gain.astype(jnp.float32)[None]).astype(jnp.bfloat16)
    in_weight, normed = lax.optimization_barrier((in_weight, normed))
    gathered = lax.all_gather(normed, ("y", "core"), axis=0, tiled=True)
    weight_t = in_weight.transpose(1, 2, 0).reshape(3 * channels, width)
    piece, weight_t = lax.optimization_barrier((piece, weight_t))
    ends = cut(jnp.where(top, depth - 1, 0)), cut(jnp.where(top, depth - 2, 1))
    piece, *ends = lax.optimization_barrier((piece, *ends))
    columns = spread_columns(piece, ends)

    small = jnp.concatenate(
        [short_filter.reshape(3 * taps, channels), long_filter.reshape(-1, channels)], axis=0
    )
    small = swap(small, "z_hi")
    other_short, other_long = small[: 3 * taps], small[3 * taps :].reshape(groups, span)

    next_half = [(i, i + 1) for i in range(contexts * lax.axis_size("z_hi") - 1)]

    def halo_of(projected, short):
        return lax.ppermute(tail_of(projected, short, starts), ("z_lo", "x", "z_hi"), next_half)

    own_short = short_filter.reshape(3 * taps, channels).astype(jnp.float32)
    other_short = other_short.astype(jnp.float32)
    own_projected = lax.dot_general(
        gathered, weight_t, (((1,), (1,)), ((), ())), preferred_element_type=jnp.float32
    ).astype(jnp.bfloat16)
    rows_of = [spread_rows(mine) for _, mine in columns]
    onwards = [onward for _, _, onward in rows_of]
    onwards[1], onwards[2], own_projected = lax.optimization_barrier((onwards[1], onwards[2], own_projected))
    pieces, places = [], []
    for (by, mine), (below, above, _), onward in zip(columns, rows_of, onwards):
        pieces += [mine, below, above, lax.ppermute(onward, ("x", "core"), fan("x"))]
        places += places_of(by)
    half = len(pieces) // 2
    first_sum = add_product(gathered, pieces[:half], places[:half], None, jnp.float32)
    first_sum, own_projected = lax.optimization_barrier((first_sum, own_projected))
    other_halo = halo_of(own_projected, own_short)
    own_band, other_band = banded(long_filter), banded(other_long)
    nothing = jnp.zeros((SPAN + 3 * RIM, channels), jnp.bfloat16)
    gated = mix_conv(own_projected, nothing, own_short, own_band, starts, length, None, 0)
    first_sum, gated = lax.optimization_barrier((first_sum, gated))
    other_projected = add_product(gathered, pieces[half:], places[half:], first_sum, jnp.bfloat16)
    own_halo = halo_of(other_projected, other_short)
    gated = mix_conv(other_projected, other_halo, other_short, other_band, starts, length, gated, 1)
    gated = mix_conv(own_projected, own_halo, own_short, own_band, starts, 2 * SPAN, gated, 0)
    returned = lax.all_to_all(gated, ("y", "core"), split_axis=0, concat_axis=1, tiled=True)
    returned = returned.reshape(rows, -1, 2, channels)
    own, other = returned[:, :, 0].reshape(rows, -1), returned[:, :, 1].reshape(rows, -1)
    left = jnp.where(z_hi == 0, own, other)
    right = jnp.where(z_hi == 0, other, own)
    gated = jnp.concatenate([left, right], axis=1)
    return (float_tokens + gated.astype(jnp.float32)).astype(jnp.bfloat16)


def solution(mesh):
    fine = Mesh(mesh.devices.reshape(4, 4, 2, 4, 2), AXES)
    context, tensor = ("z_lo", "x"), ("z_hi", "y", "core")
    in_specs = (
        P(context + tensor, None),
        P(),
        P(None, None, tensor),
        P(None, None, tensor),
        P(tensor, None),
        P(context),
    )
    return jax.shard_map(
        per_device, mesh=fine, in_specs=in_specs, out_specs=P(context + tensor, None), check_vma=False
    )
```

```python
import functools

import jax
import jax.numpy as jnp
from jax import lax
from jax.experimental import pallas as pl
from jax.experimental.pallas import tpu as pltpu
from jax.sharding import Mesh
from jax.sharding import PartitionSpec as P

AXES = ("z_lo", "x", "z_hi", "y", "core")
SPAN = 128
RIM = 16


def swap(value, axis):
    return lax.ppermute(value, axis, [(0, 1), (1, 0)])


def shift(value, axis, by):
    size = lax.axis_size(axis)
    return lax.ppermute(value, axis, [(i, (i + by) % size) for i in range(size)])


def fan(axis):
    size = lax.axis_size(axis)
    return [(2 * i + c, 2 * ((i + 1 - 2 * c) % size) + c) for i in range(size) for c in range(2)]


def band_kernel(taps, band):
    groups, span = taps.shape
    for g in range(groups):
        row = jnp.concatenate([taps[g : g + 1, :], jnp.zeros((1, span), jnp.float32)], axis=1)
        rows = jnp.broadcast_to(row, (2 * span, 2 * span))
        moved = pltpu.roll(rows, 0, axis=1, stride=1, stride_axis=0)
        band[g] = moved[:, span:].astype(band.dtype)


def banded(long_filter):
    groups, span = long_filter.shape
    vmem = pl.BlockSpec(memory_space=pltpu.VMEM)
    return pl.pallas_call(
        band_kernel,
        out_shape=jax.ShapeDtypeStruct((groups, 2 * span, span), jnp.bfloat16),
        in_specs=[vmem],
        out_specs=vmem,
        compiler_params=pltpu.CompilerParams(vmem_limit_bytes=16 << 20),
        cost_estimate=pl.CostEstimate(flops=2_000_000_000, bytes_accessed=1_000_000, transcendentals=0),
    )(long_filter.astype(jnp.float32))


def across(value, by):
    size = lax.axis_size("z_lo")
    pairs = [(2 * i + h, 2 * ((i + by) % size) + 1 - h) for i in range(size) for h in range(2)]
    return lax.ppermute(value, ("z_lo", "z_hi"), pairs)


def ring(value, by):
    size = lax.axis_size("z_lo")
    pairs = []
    for i in range(size):
        for h in range(2):
            to = (h * size + i + by) % (2 * size)
            pairs.append((2 * i + h, 2 * (to % size) + to // size))
    return lax.ppermute(value, ("z_lo", "z_hi"), pairs)


def spread_columns(piece, ends):
    z_lo = lax.axis_index("z_lo")
    size = lax.axis_size("z_lo")
    top, bottom = z_lo == size - 1, z_lo == 0
    up = ring(jnp.where(top, ends[0], piece), 1)
    down = ring(jnp.where(bottom, ends[0], piece), -1)
    pairs = []
    for h in range(2):
        pairs += [(2 * 1 + h, 2 * 2 + h), (2 * 2 + h, 2 * 1 + h)]
        pairs += [(2 * 0 + h, 2 * 3 + 1 - h), (2 * 3 + h, 2 * 0 + 1 - h)]
    onward = jnp.where(jnp.logical_or(top, bottom), ends[1], jnp.where(z_lo == 1, up, down))
    opposite = lax.ppermute(onward, ("z_lo", "z_hi"), pairs)
    return (0, piece), (1, up), (-1, down), (2, opposite)


def spread_rows(mine):
    below, above = shift(mine, "x", 1), shift(mine, "x", -1)
    return below, above, jnp.where(lax.axis_index("core") == 0, below, above)


def places_of(by):
    z_lo, x = lax.axis_index("z_lo"), lax.axis_index("x")
    depth, size = lax.axis_size("z_lo"), lax.axis_size("x")
    first = (z_lo - by + depth) % depth * size
    return [first + x, first + (x + size - 1) % size, first + (x + 1) % size, first + (x + 2) % size]


def add_product_kernel(count, places, left, *refs):
    rights, rest = refs[:count], refs[count:]
    deep = rights[0].shape[0]
    step = 256
    for first in range(0, left.shape[0], step):
        rows = slice(first, first + step)
        total = rest[0][rows, :] if len(rest) == 2 else None
        for n, right in enumerate(rights):
            columns = pl.ds(pl.multiple_of(places[n] * deep, deep), deep)
            term = jnp.dot(left[rows, columns], right[...], preferred_element_type=jnp.float32)
            total = term if total is None else total + term
        rest[-1][rows, :] = total.astype(rest[-1].dtype)


def add_product(left, pieces, places, total, dtype):
    length = left.shape[0]
    deep, wide = pieces[0].shape
    count = len(pieces)
    vmem = pl.BlockSpec(memory_space=pltpu.VMEM)
    given = [left, *pieces] + ([] if total is None else [total])
    return pl.pallas_call(
        functools.partial(add_product_kernel, count),
        out_shape=jax.ShapeDtypeStruct((length, wide), dtype),
        in_specs=[pl.BlockSpec(memory_space=pltpu.SMEM)] + [vmem] * len(given),
        out_specs=vmem,
        compiler_params=pltpu.CompilerParams(vmem_limit_bytes=24 << 20),
        cost_estimate=pl.CostEstimate(
            flops=2 * length * deep * wide * count, bytes_accessed=8_000_000, transcendentals=0
        ),
    )(jnp.stack(places).astype(jnp.int32), *given)


def add_returned_kernel(half, tokens, returned, out):
    rows = tokens.shape[0]
    sources = returned.shape[0] // rows
    channels = returned.shape[1] // 2
    for side in range(2):
        for n in range(sources):
            first = ((half[0] if side == 0 else 1 - half[0]) * sources + n) * channels
            columns = pl.ds(pl.multiple_of(first, channels), channels)
            gated = returned[n * rows : (n + 1) * rows, side * channels : (side + 1) * channels]
            total = tokens[:, columns].astype(jnp.float32) + gated.astype(jnp.float32)
            out[:, columns] = total.astype(out.dtype)


def add_returned(tokens, returned, half):
    vmem = pl.BlockSpec(memory_space=pltpu.VMEM)
    return pl.pallas_call(
        add_returned_kernel,
        out_shape=jax.ShapeDtypeStruct(tokens.shape, jnp.bfloat16),
        in_specs=[pl.BlockSpec(memory_space=pltpu.SMEM), vmem, vmem],
        out_specs=vmem,
        compiler_params=pltpu.CompilerParams(vmem_limit_bytes=16 << 20),
        cost_estimate=pl.CostEstimate(flops=1_000_000, bytes_accessed=3_000_000, transcendentals=0),
    )(half[None].astype(jnp.int32), tokens, returned)


def mix_conv_kernel(
    flags, proj, halo, short, band, start_col, start_row, into, out, key_value_t, query, conv_t
):
    del into
    length, channels = out.shape
    groups = band.shape[0]
    share = channels // groups
    blocks = length // SPAN
    taps = short.shape[0] // 3
    key_value_t[:, 0:SPAN] = halo[0:SPAN, :].astype(jnp.float32).T.astype(jnp.bfloat16)
    for b in range(blocks):
        rows = slice(b * SPAN, (b + 1) * SPAN)
        starts = start_col[rows, :]
        places = b * SPAN + lax.broadcasted_iota(jnp.int32, (SPAN, 1), 0)
        mixed = []
        for m in range(3):
            cols = slice(m * channels, (m + 1) * channels)
            if b == 0:
                before = halo[SPAN + m * RIM : SPAN + (m + 1) * RIM, :]
            else:
                before = proj[b * SPAN - RIM : b * SPAN, cols]
            both = jnp.concatenate([before, proj[rows, cols]], axis=0).astype(jnp.float32)
            total = None
            for s in range(taps):
                term = short[m * taps + s : m * taps + s + 1, :] * both[RIM - s : RIM - s + SPAN]
                term = jnp.where(places - s >= starts, term, 0.0)
                total = term if total is None else total + term
            mixed.append(total)
        query[rows, :] = mixed[0]
        key_value_t[:, (b + 1) * SPAN : (b + 2) * SPAN] = (mixed[1] * mixed[2]).T.astype(jnp.bfloat16)
    for g in range(groups):
        rows = slice(g * share, (g + 1) * share)
        windows = jnp.concatenate(
            [key_value_t[rows, b * SPAN : (b + 2) * SPAN] for b in range(blocks)], axis=0
        )
        sums = jnp.dot(windows, band[g], preferred_element_type=jnp.float32)
        for b in range(blocks):
            conv_t[rows, b * SPAN : (b + 1) * SPAN] = sums[b * share : (b + 1) * share]
    for b in range(blocks):

        @pl.when(flags[b] > 0)
        def _(b=b):
            inputs = (b - 1) * SPAN + lax.broadcasted_iota(jnp.int32, (2 * SPAN, SPAN), 0)
            kept = (inputs >= start_row[:, b * SPAN : (b + 1) * SPAN])

            def one_group(g, _):
                rows = pl.ds(pl.multiple_of(g * share, share), share)
                weights = jnp.where(kept, band[g].astype(jnp.float32), 0.0).astype(jnp.bfloat16)
                conv_t[rows, b * SPAN : (b + 1) * SPAN] = jnp.dot(
                    key_value_t[rows, b * SPAN : (b + 2) * SPAN],
                    weights,
                    preferred_element_type=jnp.float32,
                )
                return 0

            lax.fori_loop(0, groups, one_group, 0, unroll=4)

    for b in range(blocks):
        rows = slice(b * SPAN, (b + 1) * SPAN)
        out[rows, :] = (query[rows, :] * conv_t[:, b * SPAN : (b + 1) * SPAN].T).astype(out.dtype)


def mix_conv(proj, halo, short, band, starts, rows, into, side):
    length, channels = proj.shape[0], proj.shape[1] // 3
    blocks = rows // SPAN
    starts = starts[:rows]
    last = starts.reshape(blocks, SPAN)[:, -1]
    flags = (last > jnp.arange(blocks, dtype=jnp.int32) * SPAN - (SPAN - 1)).astype(jnp.int32)
    given = [flags, proj, halo, short, band, starts[:, None], starts[None, :]]
    in_specs = [pl.BlockSpec(memory_space=pltpu.SMEM), pl.BlockSpec((rows, 3 * channels), lambda n: (0, 0))]
    in_specs += [pl.BlockSpec(memory_space=pltpu.VMEM)] * 5
    body = mix_conv_kernel
    aliases = {}
    if into is None:
        body = lambda *refs: mix_conv_kernel(*refs[:7], None, *refs[7:])
    else:
        aliases = {len(given): 0}
        given.append(into)
        in_specs.append(pl.BlockSpec(memory_space=pl.ANY))
    return pl.pallas_call(
        body,
        out_shape=jax.ShapeDtypeStruct((length, 2 * channels), jnp.bfloat16),
        grid=(1,),
        in_specs=in_specs,
        out_specs=pl.BlockSpec((rows, channels), lambda n: (0, side)),
        scratch_shapes=[
            pltpu.VMEM((channels, rows + SPAN), jnp.bfloat16),
            pltpu.VMEM((rows, channels), jnp.float32),
            pltpu.VMEM((channels, rows), jnp.float32),
        ],
        input_output_aliases=aliases,
        compiler_params=pltpu.CompilerParams(vmem_limit_bytes=24 << 20),
        cost_estimate=pl.CostEstimate(flops=rows * 6_000_000, bytes_accessed=4_000_000, transcendentals=0),
    )(*given)


def tail_of(proj, short, starts):
    length = proj.shape[0]
    channels = proj.shape[1] // 3
    taps = short.shape[0] // 3
    places = jnp.arange(length - SPAN, length, dtype=jnp.int32)
    mixed = []
    for m in (1, 2):
        total = jnp.zeros((SPAN, channels), jnp.float32)
        for s in range(taps):
            rows = proj[length - SPAN - s : length - s, m * channels : (m + 1) * channels].astype(jnp.float32)
            kept = (places - s >= starts[length - SPAN :])[:, None]
            total = total + jnp.where(kept, short[m * taps + s][None] * rows, 0.0)
        mixed.append(total)
    key_value = (mixed[0] * mixed[1]).astype(jnp.bfloat16)
    rims = [proj[length - RIM :, m * channels : (m + 1) * channels] for m in range(3)]
    return jnp.concatenate([key_value, *rims], axis=0)


def per_device(tokens, norm_gain, in_weight, short_filter, long_filter, doc_start):
    rows, width = tokens.shape
    channels = in_weight.shape[2]
    groups, span = long_filter.shape
    taps = short_filter.shape[1]
    z_lo, x, z_hi = lax.axis_index("z_lo"), lax.axis_index("x"), lax.axis_index("z_hi")
    contexts = lax.axis_size("z_lo") * lax.axis_size("x")
    context = z_lo * lax.axis_size("x") + x
    length = rows * lax.axis_size("y") * lax.axis_size("core")
    starts = lax.dynamic_slice_in_dim(doc_start, z_hi * length, length, 0)
    starts = starts - (context * lax.axis_size("z_hi") + z_hi) * length

    deep = width // contexts
    depth = lax.axis_size("z_lo")

    def cut(quarter):
        first = (quarter * lax.axis_size("x") + x) * deep
        return lax.dynamic_slice_in_dim(in_weight, first, deep, 0).reshape(deep, 3 * channels)

    piece, tokens = lax.optimization_barrier((cut((z_lo + 2) % depth), tokens))
    piece = across(piece, 2)
    top = z_lo == depth - 1

    float_tokens = tokens.astype(jnp.float32)
    scale_rows = lax.rsqrt(jnp.mean(float_tokens * float_tokens, axis=-1, keepdims=True) + 1e-06)
    normed = (float_tokens * scale_rows * norm_gain.astype(jnp.float32)[None]).astype(jnp.bfloat16)
    in_weight, normed = lax.optimization_barrier((in_weight, normed))
    gathered = lax.all_gather(normed, ("y", "core"), axis=0, tiled=True)
    weight_t = in_weight.transpose(1, 2, 0).reshape(3 * channels, width)
    piece, weight_t = lax.optimization_barrier((piece, weight_t))
    ends = cut(jnp.where(top, depth - 1, 0)), cut(jnp.where(top, depth - 2, 1))
    piece, *ends = lax.optimization_barrier((piece, *ends))
    columns = spread_columns(piece, ends)

    small = jnp.concatenate(
        [short_filter.reshape(3 * taps, channels), long_filter.reshape(-1, channels)], axis=0
    )
    small = swap(small, "z_hi")
    other_short, other_long = small[: 3 * taps], small[3 * taps :].reshape(groups, span)

    next_half = [(i, i + 1) for i in range(contexts * lax.axis_size("z_hi") - 1)]

    def halo_of(projected, short):
        return lax.ppermute(tail_of(projected, short, starts), ("z_lo", "x", "z_hi"), next_half)

    own_short = short_filter.reshape(3 * taps, channels).astype(jnp.float32)
    other_short = other_short.astype(jnp.float32)
    own_projected = lax.dot_general(
        gathered, weight_t, (((1,), (1,)), ((), ())), preferred_element_type=jnp.float32
    ).astype(jnp.bfloat16)
    rows_of = [spread_rows(mine) for _, mine in columns]
    onwards = [onward for _, _, onward in rows_of]
    onwards[3], own_projected = lax.optimization_barrier((onwards[3], own_projected))
    pieces, places = [], []
    for (by, mine), (below, above, _), onward in zip(columns, rows_of, onwards):
        pieces += [mine, below, above, lax.ppermute(onward, ("x", "core"), fan("x"))]
        places += places_of(by)
    half = len(pieces) // 2
    first_sum = add_product(gathered, pieces[:half], places[:half], None, jnp.float32)
    first_sum, own_projected = lax.optimization_barrier((first_sum, own_projected))
    other_halo = halo_of(own_projected, own_short)
    own_band, other_band = banded(long_filter), banded(other_long)
    nothing = jnp.zeros((SPAN + 3 * RIM, channels), jnp.bfloat16)
    gated = mix_conv(own_projected, nothing, own_short, own_band, starts, length, None, 0)
    first_sum, gated = lax.optimization_barrier((first_sum, gated))
    other_projected = add_product(gathered, pieces[half:], places[half:], first_sum, jnp.bfloat16)
    own_halo = halo_of(other_projected, other_short)
    gated = mix_conv(other_projected, other_halo, other_short, other_band, starts, length, gated, 1)
    gated = mix_conv(own_projected, own_halo, own_short, own_band, starts, 2 * SPAN, gated, 0)
    returned = lax.all_to_all(gated, ("y", "core"), split_axis=0, concat_axis=0, tiled=True)
    return add_returned(tokens, returned, z_hi)


def solution(mesh):
    fine = Mesh(mesh.devices.reshape(4, 4, 2, 4, 2), AXES)
    context, tensor = ("z_lo", "x"), ("z_hi", "y", "core")
    in_specs = (
        P(context + tensor, None),
        P(),
        P(None, None, tensor),
        P(None, None, tensor),
        P(tensor, None),
        P(context),
    )
    return jax.shard_map(
        per_device, mesh=fine, in_specs=in_specs, out_specs=P(context + tensor, None), check_vma=False
    )
```

```python
import functools

import jax
import jax.numpy as jnp
from jax import lax
from jax.experimental import pallas as pl
from jax.experimental.pallas import tpu as pltpu
from jax.sharding import Mesh
from jax.sharding import PartitionSpec as P

AXES = ("z_lo", "x", "z_hi", "y", "core")
SPAN = 128
RIM = 16


def swap(value, axis):
    return lax.ppermute(value, axis, [(0, 1), (1, 0)])


def shift(value, axis, by):
    size = lax.axis_size(axis)
    return lax.ppermute(value, axis, [(i, (i + by) % size) for i in range(size)])


def fan(axis):
    size = lax.axis_size(axis)
    return [(2 * i + c, 2 * ((i + 1 - 2 * c) % size) + c) for i in range(size) for c in range(2)]


def band_kernel(taps, band):
    groups, span = taps.shape
    for g in range(groups):
        row = jnp.concatenate([taps[g : g + 1, :], jnp.zeros((1, span), jnp.float32)], axis=1)
        rows = jnp.broadcast_to(row, (2 * span, 2 * span))
        moved = pltpu.roll(rows, 0, axis=1, stride=1, stride_axis=0)
        band[g] = moved[:, span:].astype(band.dtype)


def banded(long_filter):
    groups, span = long_filter.shape
    vmem = pl.BlockSpec(memory_space=pltpu.VMEM)
    return pl.pallas_call(
        band_kernel,
        out_shape=jax.ShapeDtypeStruct((groups, 2 * span, span), jnp.bfloat16),
        in_specs=[vmem],
        out_specs=vmem,
        compiler_params=pltpu.CompilerParams(vmem_limit_bytes=16 << 20),
        cost_estimate=pl.CostEstimate(flops=2_000_000_000, bytes_accessed=1_000_000, transcendentals=0),
    )(long_filter.astype(jnp.float32))


def across(value, by):
    size = lax.axis_size("z_lo")
    pairs = [(2 * i + h, 2 * ((i + by) % size) + 1 - h) for i in range(size) for h in range(2)]
    return lax.ppermute(value, ("z_lo", "z_hi"), pairs)


def ring(value, by):
    size = lax.axis_size("z_lo")
    pairs = []
    for i in range(size):
        for h in range(2):
            to = (h * size + i + by) % (2 * size)
            pairs.append((2 * i + h, 2 * (to % size) + to // size))
    return lax.ppermute(value, ("z_lo", "z_hi"), pairs)


def spread_columns(piece, ends):
    z_lo = lax.axis_index("z_lo")
    size = lax.axis_size("z_lo")
    top, bottom = z_lo == size - 1, z_lo == 0
    up = ring(jnp.where(top, ends[0], piece), 1)
    down = ring(jnp.where(bottom, ends[0], piece), -1)
    pairs = []
    for h in range(2):
        pairs += [(2 * 1 + h, 2 * 2 + h), (2 * 2 + h, 2 * 1 + h)]
        pairs += [(2 * 0 + h, 2 * 3 + 1 - h), (2 * 3 + h, 2 * 0 + 1 - h)]
    onward = jnp.where(jnp.logical_or(top, bottom), ends[1], jnp.where(z_lo == 1, up, down))
    opposite = lax.ppermute(onward, ("z_lo", "z_hi"), pairs)
    return (0, piece), (1, up), (-1, down), (2, opposite)


def spread_rows(mine):
    below, above = shift(mine, "x", 1), shift(mine, "x", -1)
    return below, above, jnp.where(lax.axis_index("core") == 0, below, above)


def places_of(by):
    z_lo, x = lax.axis_index("z_lo"), lax.axis_index("x")
    depth, size = lax.axis_size("z_lo"), lax.axis_size("x")
    first = (z_lo - by + depth) % depth * size
    return [first + x, first + (x + size - 1) % size, first + (x + 1) % size, first + (x + 2) % size]


def add_product_kernel(count, places, left, *refs):
    rights, rest = refs[:count], refs[count:]
    deep = rights[0].shape[0]
    step = 256
    for first in range(0, left.shape[0], step):
        rows = slice(first, first + step)
        total = rest[0][rows, :] if len(rest) == 2 else None
        for n, right in enumerate(rights):
            columns = pl.ds(pl.multiple_of(places[n] * deep, deep), deep)
            term = jnp.dot(left[rows, columns], right[...], preferred_element_type=jnp.float32)
            total = term if total is None else total + term
        rest[-1][rows, :] = total.astype(rest[-1].dtype)


def add_product(left, pieces, places, total, dtype):
    length = left.shape[0]
    deep, wide = pieces[0].shape
    count = len(pieces)
    vmem = pl.BlockSpec(memory_space=pltpu.VMEM)
    given = [left, *pieces] + ([] if total is None else [total])
    return pl.pallas_call(
        functools.partial(add_product_kernel, count),
        out_shape=jax.ShapeDtypeStruct((length, wide), dtype),
        in_specs=[pl.BlockSpec(memory_space=pltpu.SMEM)] + [vmem] * len(given),
        out_specs=vmem,
        compiler_params=pltpu.CompilerParams(vmem_limit_bytes=24 << 20),
        cost_estimate=pl.CostEstimate(
            flops=2 * length * deep * wide * count, bytes_accessed=8_000_000, transcendentals=0
        ),
    )(jnp.stack(places).astype(jnp.int32), *given)


def add_returned_kernel(half, tokens, returned, out):
    rows = tokens.shape[0]
    sources = returned.shape[0] // rows
    channels = returned.shape[1] // 2
    for side in range(2):
        for n in range(sources):
            first = ((half[0] if side == 0 else 1 - half[0]) * sources + n) * channels
            columns = pl.ds(pl.multiple_of(first, channels), channels)
            gated = returned[n * rows : (n + 1) * rows, side * channels : (side + 1) * channels]
            total = tokens[:, columns].astype(jnp.float32) + gated.astype(jnp.float32)
            out[:, columns] = total.astype(out.dtype)


def add_returned(tokens, returned, half):
    vmem = pl.BlockSpec(memory_space=pltpu.VMEM)
    return pl.pallas_call(
        add_returned_kernel,
        out_shape=jax.ShapeDtypeStruct(tokens.shape, jnp.bfloat16),
        in_specs=[pl.BlockSpec(memory_space=pltpu.SMEM), vmem, vmem],
        out_specs=vmem,
        compiler_params=pltpu.CompilerParams(vmem_limit_bytes=16 << 20),
        cost_estimate=pl.CostEstimate(flops=1_000_000, bytes_accessed=3_000_000, transcendentals=0),
    )(half[None].astype(jnp.int32), tokens, returned)


def mix_conv_kernel(
    flags, proj, halo, short, band, start_col, start_row, into, out, key_value_t, query, conv_t
):
    del into
    length, channels = out.shape
    groups = band.shape[0]
    share = channels // groups
    blocks = length // SPAN
    taps = short.shape[0] // 3
    key_value_t[:, 0:SPAN] = halo[0:SPAN, :].astype(jnp.float32).T.astype(jnp.bfloat16)
    for b in range(blocks):
        rows = slice(b * SPAN, (b + 1) * SPAN)
        starts = start_col[rows, :]
        places = b * SPAN + lax.broadcasted_iota(jnp.int32, (SPAN, 1), 0)
        mixed = []
        for m in range(3):
            cols = slice(m * channels, (m + 1) * channels)
            if b == 0:
                before = halo[SPAN + m * RIM : SPAN + (m + 1) * RIM, :]
            else:
                before = proj[b * SPAN - RIM : b * SPAN, cols]
            both = jnp.concatenate([before, proj[rows, cols]], axis=0).astype(jnp.float32)
            total = None
            for s in range(taps):
                term = short[m * taps + s : m * taps + s + 1, :] * both[RIM - s : RIM - s + SPAN]
                term = jnp.where(places - s >= starts, term, 0.0)
                total = term if total is None else total + term
            mixed.append(total)
        query[rows, :] = mixed[0]
        key_value_t[:, (b + 1) * SPAN : (b + 2) * SPAN] = (mixed[1] * mixed[2]).T.astype(jnp.bfloat16)
    for g in range(groups):
        rows = slice(g * share, (g + 1) * share)
        windows = jnp.concatenate(
            [key_value_t[rows, b * SPAN : (b + 2) * SPAN] for b in range(blocks)], axis=0
        )
        sums = jnp.dot(windows, band[g], preferred_element_type=jnp.float32)
        for b in range(blocks):
            conv_t[rows, b * SPAN : (b + 1) * SPAN] = sums[b * share : (b + 1) * share]
    for b in range(blocks):

        @pl.when(flags[b] > 0)
        def _(b=b):
            inputs = (b - 1) * SPAN + lax.broadcasted_iota(jnp.int32, (2 * SPAN, SPAN), 0)
            kept = (inputs >= start_row[:, b * SPAN : (b + 1) * SPAN])

            def one_group(g, _):
                rows = pl.ds(pl.multiple_of(g * share, share), share)
                weights = jnp.where(kept, band[g].astype(jnp.float32), 0.0).astype(jnp.bfloat16)
                conv_t[rows, b * SPAN : (b + 1) * SPAN] = jnp.dot(
                    key_value_t[rows, b * SPAN : (b + 2) * SPAN],
                    weights,
                    preferred_element_type=jnp.float32,
                )
                return 0

            lax.fori_loop(0, groups, one_group, 0, unroll=4)

    for b in range(blocks):
        rows = slice(b * SPAN, (b + 1) * SPAN)
        out[rows, :] = (query[rows, :] * conv_t[:, b * SPAN : (b + 1) * SPAN].T).astype(out.dtype)


def mix_conv(proj, halo, short, band, starts, rows, into, side):
    length, channels = proj.shape[0], proj.shape[1] // 3
    blocks = rows // SPAN
    starts = starts[:rows]
    last = starts.reshape(blocks, SPAN)[:, -1]
    flags = (last > jnp.arange(blocks, dtype=jnp.int32) * SPAN - (SPAN - 1)).astype(jnp.int32)
    given = [flags, proj, halo, short, band, starts[:, None], starts[None, :]]
    in_specs = [pl.BlockSpec(memory_space=pltpu.SMEM), pl.BlockSpec((rows, 3 * channels), lambda n: (0, 0))]
    in_specs += [pl.BlockSpec(memory_space=pltpu.VMEM)] * 5
    body = mix_conv_kernel
    aliases = {}
    if into is None:
        body = lambda *refs: mix_conv_kernel(*refs[:7], None, *refs[7:])
    else:
        aliases = {len(given): 0}
        given.append(into)
        in_specs.append(pl.BlockSpec(memory_space=pl.ANY))
    return pl.pallas_call(
        body,
        out_shape=jax.ShapeDtypeStruct((length, 2 * channels), jnp.bfloat16),
        grid=(1,),
        in_specs=in_specs,
        out_specs=pl.BlockSpec((rows, channels), lambda n: (0, side)),
        scratch_shapes=[
            pltpu.VMEM((channels, rows + SPAN), jnp.bfloat16),
            pltpu.VMEM((rows, channels), jnp.float32),
            pltpu.VMEM((channels, rows), jnp.float32),
        ],
        input_output_aliases=aliases,
        compiler_params=pltpu.CompilerParams(vmem_limit_bytes=24 << 20),
        cost_estimate=pl.CostEstimate(flops=rows * 6_000_000, bytes_accessed=4_000_000, transcendentals=0),
    )(*given)


def tail_of(proj, short, starts):
    length = proj.shape[0]
    channels = proj.shape[1] // 3
    taps = short.shape[0] // 3
    places = jnp.arange(length - SPAN, length, dtype=jnp.int32)
    mixed = []
    for m in (1, 2):
        total = jnp.zeros((SPAN, channels), jnp.float32)
        for s in range(taps):
            rows = proj[length - SPAN - s : length - s, m * channels : (m + 1) * channels].astype(jnp.float32)
            kept = (places - s >= starts[length - SPAN :])[:, None]
            total = total + jnp.where(kept, short[m * taps + s][None] * rows, 0.0)
        mixed.append(total)
    key_value = (mixed[0] * mixed[1]).astype(jnp.bfloat16)
    rims = [proj[length - RIM :, m * channels : (m + 1) * channels] for m in range(3)]
    return jnp.concatenate([key_value, *rims], axis=0)


def per_device(tokens, norm_gain, in_weight, short_filter, long_filter, doc_start):
    rows, width = tokens.shape
    channels = in_weight.shape[2]
    groups, span = long_filter.shape
    taps = short_filter.shape[1]
    z_lo, x, z_hi = lax.axis_index("z_lo"), lax.axis_index("x"), lax.axis_index("z_hi")
    contexts = lax.axis_size("z_lo") * lax.axis_size("x")
    context = z_lo * lax.axis_size("x") + x
    length = rows * lax.axis_size("y") * lax.axis_size("core")
    starts = lax.dynamic_slice_in_dim(doc_start, z_hi * length, length, 0)
    starts = starts - (context * lax.axis_size("z_hi") + z_hi) * length

    deep = width // contexts
    depth = lax.axis_size("z_lo")

    def cut(quarter):
        first = (quarter * lax.axis_size("x") + x) * deep
        return lax.dynamic_slice_in_dim(in_weight, first, deep, 0).reshape(deep, 3 * channels)

    piece, tokens = lax.optimization_barrier((cut((z_lo + 2) % depth), tokens))
    piece = across(piece, 2)
    top = z_lo == depth - 1

    float_tokens = tokens.astype(jnp.float32)
    scale_rows = lax.rsqrt(jnp.mean(float_tokens * float_tokens, axis=-1, keepdims=True) + 1e-06)
    normed = (float_tokens * scale_rows * norm_gain.astype(jnp.float32)[None]).astype(jnp.bfloat16)
    in_weight, normed = lax.optimization_barrier((in_weight, normed))
    gathered = lax.all_gather(normed, ("y", "core"), axis=0, tiled=True)
    weight_t = in_weight.transpose(1, 2, 0).reshape(3 * channels, width)
    piece, weight_t = lax.optimization_barrier((piece, weight_t))
    ends = cut(jnp.where(top, depth - 1, 0)), cut(jnp.where(top, depth - 2, 1))
    piece, *ends = lax.optimization_barrier((piece, *ends))
    columns = spread_columns(piece, ends)

    small = jnp.concatenate(
        [short_filter.reshape(3 * taps, channels), long_filter.reshape(-1, channels)], axis=0
    )
    small = swap(small, "z_hi")
    other_short, other_long = small[: 3 * taps], small[3 * taps :].reshape(groups, span)

    next_half = [(i, i + 1) for i in range(contexts * lax.axis_size("z_hi") - 1)]

    def halo_of(projected, short):
        return lax.ppermute(tail_of(projected, short, starts), ("z_lo", "x", "z_hi"), next_half)

    own_short = short_filter.reshape(3 * taps, channels).astype(jnp.float32)
    other_short = other_short.astype(jnp.float32)
    own_projected = lax.dot_general(
        gathered, weight_t, (((1,), (1,)), ((), ())), preferred_element_type=jnp.float32
    ).astype(jnp.bfloat16)
    rows_of = [spread_rows(mine) for _, mine in columns]
    onwards = [onward for _, _, onward in rows_of]
    onwards[2], own_projected = lax.optimization_barrier((onwards[2], own_projected))
    pieces, places = [], []
    for (by, mine), (below, above, _), onward in zip(columns, rows_of, onwards):
        pieces += [mine, below, above, lax.ppermute(onward, ("x", "core"), fan("x"))]
        places += places_of(by)
    half = len(pieces) // 2
    first_sum = add_product(gathered, pieces[:half], places[:half], None, jnp.float32)
    first_sum, own_projected = lax.optimization_barrier((first_sum, own_projected))
    other_halo = halo_of(own_projected, own_short)
    own_band, other_band = banded(long_filter), banded(other_long)
    nothing = jnp.zeros((SPAN + 3 * RIM, channels), jnp.bfloat16)
    gated = mix_conv(own_projected, nothing, own_short, own_band, starts, length, None, 0)
    first_sum, gated = lax.optimization_barrier((first_sum, gated))
    other_projected = add_product(gathered, pieces[half:], places[half:], first_sum, jnp.bfloat16)
    own_halo = halo_of(other_projected, other_short)
    gated = mix_conv(other_projected, other_halo, other_short, other_band, starts, length, gated, 1)
    gated = mix_conv(own_projected, own_halo, own_short, own_band, starts, 2 * SPAN, gated, 0)
    returned = lax.all_to_all(gated, ("y", "core"), split_axis=0, concat_axis=0, tiled=True)
    return add_returned(tokens, returned, z_hi)


def solution(mesh):
    fine = Mesh(mesh.devices.reshape(4, 4, 2, 4, 2), AXES)
    context, tensor = ("z_lo", "x"), ("z_hi", "y", "core")
    in_specs = (
        P(context + tensor, None),
        P(),
        P(None, None, tensor),
        P(None, None, tensor),
        P(tensor, None),
        P(context),
    )
    return jax.shard_map(
        per_device, mesh=fine, in_specs=in_specs, out_specs=P(context + tensor, None), check_vma=False
    )
```

```python
import functools

import jax
import jax.numpy as jnp
from jax import lax
from jax.experimental import pallas as pl
from jax.experimental.pallas import tpu as pltpu
from jax.sharding import Mesh
from jax.sharding import PartitionSpec as P

AXES = ("z_lo", "x", "z_hi", "y", "core")
SPAN = 128
RIM = 16


def swap(value, axis):
    return lax.ppermute(value, axis, [(0, 1), (1, 0)])


def shift(value, axis, by):
    size = lax.axis_size(axis)
    return lax.ppermute(value, axis, [(i, (i + by) % size) for i in range(size)])


def fan(axis):
    size = lax.axis_size(axis)
    return [(2 * i + c, 2 * ((i + 1 - 2 * c) % size) + c) for i in range(size) for c in range(2)]


def band_kernel(taps, band):
    groups, span = taps.shape
    for g in range(groups):
        row = jnp.concatenate([taps[g : g + 1, :], jnp.zeros((1, span), jnp.float32)], axis=1)
        rows = jnp.broadcast_to(row, (2 * span, 2 * span))
        moved = pltpu.roll(rows, 0, axis=1, stride=1, stride_axis=0)
        band[g] = moved[:, span:].astype(band.dtype)


def banded(long_filter):
    groups, span = long_filter.shape
    vmem = pl.BlockSpec(memory_space=pltpu.VMEM)
    return pl.pallas_call(
        band_kernel,
        out_shape=jax.ShapeDtypeStruct((groups, 2 * span, span), jnp.bfloat16),
        in_specs=[vmem],
        out_specs=vmem,
        compiler_params=pltpu.CompilerParams(vmem_limit_bytes=16 << 20),
        cost_estimate=pl.CostEstimate(flops=2_000_000_000, bytes_accessed=1_000_000, transcendentals=0),
    )(long_filter.astype(jnp.float32))


def across(value, by):
    size = lax.axis_size("z_lo")
    pairs = [(2 * i + h, 2 * ((i + by) % size) + 1 - h) for i in range(size) for h in range(2)]
    return lax.ppermute(value, ("z_lo", "z_hi"), pairs)


def ring(value, by):
    size = lax.axis_size("z_lo")
    pairs = []
    for i in range(size):
        for h in range(2):
            to = (h * size + i + by) % (2 * size)
            pairs.append((2 * i + h, 2 * (to % size) + to // size))
    return lax.ppermute(value, ("z_lo", "z_hi"), pairs)


def spread_columns(piece, ends):
    z_lo = lax.axis_index("z_lo")
    size = lax.axis_size("z_lo")
    top, bottom = z_lo == size - 1, z_lo == 0
    up = ring(jnp.where(top, ends[0], piece), 1)
    down = ring(jnp.where(bottom, ends[0], piece), -1)
    pairs = []
    for h in range(2):
        pairs += [(2 * 1 + h, 2 * 2 + h), (2 * 2 + h, 2 * 1 + h)]
        pairs += [(2 * 0 + h, 2 * 3 + 1 - h), (2 * 3 + h, 2 * 0 + 1 - h)]
    onward = jnp.where(jnp.logical_or(top, bottom), ends[1], jnp.where(z_lo == 1, up, down))
    opposite = lax.ppermute(onward, ("z_lo", "z_hi"), pairs)
    return (0, piece), (1, up), (-1, down), (2, opposite)


def spread_rows(mine):
    below, above = shift(mine, "x", 1), shift(mine, "x", -1)
    return below, above, jnp.where(lax.axis_index("core") == 0, below, above)


def places_of(by):
    z_lo, x = lax.axis_index("z_lo"), lax.axis_index("x")
    depth, size = lax.axis_size("z_lo"), lax.axis_size("x")
    first = (z_lo - by + depth) % depth * size
    return [first + x, first + (x + size - 1) % size, first + (x + 1) % size, first + (x + 2) % size]


def add_product_kernel(count, places, left, *refs):
    rights, rest = refs[:count], refs[count:]
    deep = rights[0].shape[0]
    step = 256
    for first in range(0, left.shape[0], step):
        rows = slice(first, first + step)
        total = rest[0][rows, :] if len(rest) == 2 else None
        for n, right in enumerate(rights):
            columns = pl.ds(pl.multiple_of(places[n] * deep, deep), deep)
            term = jnp.dot(left[rows, columns], right[...], preferred_element_type=jnp.float32)
            total = term if total is None else total + term
        rest[-1][rows, :] = total.astype(rest[-1].dtype)


def add_product(left, pieces, places, total, dtype):
    length = left.shape[0]
    deep, wide = pieces[0].shape
    count = len(pieces)
    vmem = pl.BlockSpec(memory_space=pltpu.VMEM)
    given = [left, *pieces] + ([] if total is None else [total])
    return pl.pallas_call(
        functools.partial(add_product_kernel, count),
        out_shape=jax.ShapeDtypeStruct((length, wide), dtype),
        in_specs=[pl.BlockSpec(memory_space=pltpu.SMEM)] + [vmem] * len(given),
        out_specs=vmem,
        compiler_params=pltpu.CompilerParams(vmem_limit_bytes=24 << 20),
        cost_estimate=pl.CostEstimate(
            flops=2 * length * deep * wide * count, bytes_accessed=8_000_000, transcendentals=0
        ),
    )(jnp.stack(places).astype(jnp.int32), *given)


def add_returned_kernel(half, tokens, returned, out):
    rows = tokens.shape[0]
    sources = returned.shape[0] // rows
    channels = returned.shape[1] // 2
    for side in range(2):
        for n in range(sources):
            first = ((half[0] if side == 0 else 1 - half[0]) * sources + n) * channels
            columns = pl.ds(pl.multiple_of(first, channels), channels)
            gated = returned[n * rows : (n + 1) * rows, side * channels : (side + 1) * channels]
            total = tokens[:, columns].astype(jnp.float32) + gated.astype(jnp.float32)
            out[:, columns] = total.astype(out.dtype)


def add_returned(tokens, returned, half):
    vmem = pl.BlockSpec(memory_space=pltpu.VMEM)
    return pl.pallas_call(
        add_returned_kernel,
        out_shape=jax.ShapeDtypeStruct(tokens.shape, jnp.bfloat16),
        in_specs=[pl.BlockSpec(memory_space=pltpu.SMEM), vmem, vmem],
        out_specs=vmem,
        compiler_params=pltpu.CompilerParams(vmem_limit_bytes=16 << 20),
        cost_estimate=pl.CostEstimate(flops=1_000_000, bytes_accessed=3_000_000, transcendentals=0),
    )(half[None].astype(jnp.int32), tokens, returned)


def mix_conv_kernel(
    flags, proj, halo, short, band, start_col, start_row, into, out, key_value_t, query, conv_t
):
    del into
    length, channels = out.shape
    groups = band.shape[0]
    share = channels // groups
    blocks = length // SPAN
    taps = short.shape[0] // 3
    key_value_t[:, 0:SPAN] = halo[0:SPAN, :].astype(jnp.float32).T.astype(jnp.bfloat16)
    for b in range(blocks):
        rows = slice(b * SPAN, (b + 1) * SPAN)
        starts = start_col[rows, :]
        places = b * SPAN + lax.broadcasted_iota(jnp.int32, (SPAN, 1), 0)
        mixed = []
        for m in range(3):
            cols = slice(m * channels, (m + 1) * channels)
            if b == 0:
                before = halo[SPAN + m * RIM : SPAN + (m + 1) * RIM, :]
            else:
                before = proj[b * SPAN - RIM : b * SPAN, cols]
            both = jnp.concatenate([before, proj[rows, cols]], axis=0).astype(jnp.float32)
            total = None
            for s in range(taps):
                term = short[m * taps + s : m * taps + s + 1, :] * both[RIM - s : RIM - s + SPAN]
                term = jnp.where(places - s >= starts, term, 0.0)
                total = term if total is None else total + term
            mixed.append(total)
        query[rows, :] = mixed[0]
        key_value_t[:, (b + 1) * SPAN : (b + 2) * SPAN] = (mixed[1] * mixed[2]).T.astype(jnp.bfloat16)
    for g in range(groups):
        rows = slice(g * share, (g + 1) * share)
        windows = jnp.concatenate(
            [key_value_t[rows, b * SPAN : (b + 2) * SPAN] for b in range(blocks)], axis=0
        )
        sums = jnp.dot(windows, band[g], preferred_element_type=jnp.float32)
        for b in range(blocks):
            conv_t[rows, b * SPAN : (b + 1) * SPAN] = sums[b * share : (b + 1) * share]
    for b in range(blocks):

        @pl.when(flags[b] > 0)
        def _(b=b):
            inputs = (b - 1) * SPAN + lax.broadcasted_iota(jnp.int32, (2 * SPAN, SPAN), 0)
            kept = (inputs >= start_row[:, b * SPAN : (b + 1) * SPAN])

            def one_group(g, _):
                rows = pl.ds(pl.multiple_of(g * share, share), share)
                weights = jnp.where(kept, band[g].astype(jnp.float32), 0.0).astype(jnp.bfloat16)
                conv_t[rows, b * SPAN : (b + 1) * SPAN] = jnp.dot(
                    key_value_t[rows, b * SPAN : (b + 2) * SPAN],
                    weights,
                    preferred_element_type=jnp.float32,
                )
                return 0

            lax.fori_loop(0, groups, one_group, 0, unroll=4)

    for b in range(blocks):
        rows = slice(b * SPAN, (b + 1) * SPAN)
        out[rows, :] = (query[rows, :] * conv_t[:, b * SPAN : (b + 1) * SPAN].T).astype(out.dtype)


def mix_conv(proj, halo, short, band, starts, rows, into, side):
    length, channels = proj.shape[0], proj.shape[1] // 3
    blocks = rows // SPAN
    starts = starts[:rows]
    last = starts.reshape(blocks, SPAN)[:, -1]
    flags = (last > jnp.arange(blocks, dtype=jnp.int32) * SPAN - (SPAN - 1)).astype(jnp.int32)
    given = [flags, proj, halo, short, band, starts[:, None], starts[None, :]]
    in_specs = [pl.BlockSpec(memory_space=pltpu.SMEM), pl.BlockSpec((rows, 3 * channels), lambda n: (0, 0))]
    in_specs += [pl.BlockSpec(memory_space=pltpu.VMEM)] * 5
    body = mix_conv_kernel
    aliases = {}
    if into is None:
        body = lambda *refs: mix_conv_kernel(*refs[:7], None, *refs[7:])
    else:
        aliases = {len(given): 0}
        given.append(into)
        in_specs.append(pl.BlockSpec(memory_space=pl.ANY))
    return pl.pallas_call(
        body,
        out_shape=jax.ShapeDtypeStruct((length, 2 * channels), jnp.bfloat16),
        grid=(1,),
        in_specs=in_specs,
        out_specs=pl.BlockSpec((rows, channels), lambda n: (0, side)),
        scratch_shapes=[
            pltpu.VMEM((channels, rows + SPAN), jnp.bfloat16),
            pltpu.VMEM((rows, channels), jnp.float32),
            pltpu.VMEM((channels, rows), jnp.float32),
        ],
        input_output_aliases=aliases,
        compiler_params=pltpu.CompilerParams(vmem_limit_bytes=24 << 20),
        cost_estimate=pl.CostEstimate(flops=rows * 6_000_000, bytes_accessed=4_000_000, transcendentals=0),
    )(*given)


def tail_of(proj, short, starts):
    length = proj.shape[0]
    channels = proj.shape[1] // 3
    taps = short.shape[0] // 3
    places = jnp.arange(length - SPAN, length, dtype=jnp.int32)
    mixed = []
    for m in (1, 2):
        total = jnp.zeros((SPAN, channels), jnp.float32)
        for s in range(taps):
            rows = proj[length - SPAN - s : length - s, m * channels : (m + 1) * channels].astype(jnp.float32)
            kept = (places - s >= starts[length - SPAN :])[:, None]
            total = total + jnp.where(kept, short[m * taps + s][None] * rows, 0.0)
        mixed.append(total)
    key_value = (mixed[0] * mixed[1]).astype(jnp.bfloat16)
    rims = [proj[length - RIM :, m * channels : (m + 1) * channels] for m in range(3)]
    return jnp.concatenate([key_value, *rims], axis=0)


def per_device(tokens, norm_gain, in_weight, short_filter, long_filter, doc_start):
    rows, width = tokens.shape
    channels = in_weight.shape[2]
    groups, span = long_filter.shape
    taps = short_filter.shape[1]
    z_lo, x, z_hi = lax.axis_index("z_lo"), lax.axis_index("x"), lax.axis_index("z_hi")
    contexts = lax.axis_size("z_lo") * lax.axis_size("x")
    context = z_lo * lax.axis_size("x") + x
    length = rows * lax.axis_size("y") * lax.axis_size("core")
    starts = lax.dynamic_slice_in_dim(doc_start, z_hi * length, length, 0)
    starts = starts - (context * lax.axis_size("z_hi") + z_hi) * length

    deep = width // contexts
    depth = lax.axis_size("z_lo")

    def cut(quarter):
        first = (quarter * lax.axis_size("x") + x) * deep
        return lax.dynamic_slice_in_dim(in_weight, first, deep, 0).reshape(deep, 3 * channels)

    piece, tokens = lax.optimization_barrier((cut((z_lo + 2) % depth), tokens))
    piece = across(piece, 2)
    top = z_lo == depth - 1

    float_tokens = tokens.astype(jnp.float32)
    scale_rows = lax.rsqrt(jnp.mean(float_tokens * float_tokens, axis=-1, keepdims=True) + 1e-06)
    normed = (float_tokens * scale_rows * norm_gain.astype(jnp.float32)[None]).astype(jnp.bfloat16)
    in_weight, normed = lax.optimization_barrier((in_weight, normed))
    gathered = lax.all_gather(normed, ("y", "core"), axis=0, tiled=True)
    weight_t = in_weight.transpose(1, 2, 0).reshape(3 * channels, width)
    piece, weight_t = lax.optimization_barrier((piece, weight_t))
    ends = cut(jnp.where(top, depth - 1, 0)), cut(jnp.where(top, depth - 2, 1))
    piece, *ends = lax.optimization_barrier((piece, *ends))
    columns = spread_columns(piece, ends)

    small = jnp.concatenate(
        [short_filter.reshape(3 * taps, channels), long_filter.reshape(-1, channels)], axis=0
    )
    small = swap(small, "z_hi")
    other_short, other_long = small[: 3 * taps], small[3 * taps :].reshape(groups, span)

    next_half = [(i, i + 1) for i in range(contexts * lax.axis_size("z_hi") - 1)]

    def halo_of(projected, short):
        return lax.ppermute(tail_of(projected, short, starts), ("z_lo", "x", "z_hi"), next_half)

    own_short = short_filter.reshape(3 * taps, channels).astype(jnp.float32)
    other_short = other_short.astype(jnp.float32)
    own_projected = lax.dot_general(
        gathered, weight_t, (((1,), (1,)), ((), ())), preferred_element_type=jnp.float32
    ).astype(jnp.bfloat16)
    (_, mine) = columns[3]
    mine, own_projected = lax.optimization_barrier((mine, own_projected))
    columns = (*columns[:3], (columns[3][0], mine))
    rows_of = [spread_rows(mine) for _, mine in columns]
    pieces, places = [], []
    half = 8
    for n, ((by, mine), (below, above, onward)) in enumerate(zip(columns, rows_of)):
        if n == 2:
            first_sum = add_product(gathered, pieces, places, None, jnp.float32)
        if n == 3:
            onward, first_sum = lax.optimization_barrier((onward, first_sum))
        pieces += [mine, below, above, lax.ppermute(onward, ("x", "core"), fan("x"))]
        places += places_of(by)
    first_sum, own_projected = lax.optimization_barrier((first_sum, own_projected))
    other_halo = halo_of(own_projected, own_short)
    own_band, other_band = banded(long_filter), banded(other_long)
    nothing = jnp.zeros((SPAN + 3 * RIM, channels), jnp.bfloat16)
    gated = mix_conv(own_projected, nothing, own_short, own_band, starts, length, None, 0)
    first_sum, gated = lax.optimization_barrier((first_sum, gated))
    other_projected = add_product(gathered, pieces[half:], places[half:], first_sum, jnp.bfloat16)
    own_halo = halo_of(other_projected, other_short)
    gated = mix_conv(other_projected, other_halo, other_short, other_band, starts, length, gated, 1)
    gated = mix_conv(own_projected, own_halo, own_short, own_band, starts, 2 * SPAN, gated, 0)
    returned = lax.all_to_all(gated, ("y", "core"), split_axis=0, concat_axis=0, tiled=True)
    return add_returned(tokens, returned, z_hi)


def solution(mesh):
    fine = Mesh(mesh.devices.reshape(4, 4, 2, 4, 2), AXES)
    context, tensor = ("z_lo", "x"), ("z_hi", "y", "core")
    in_specs = (
        P(context + tensor, None),
        P(),
        P(None, None, tensor),
        P(None, None, tensor),
        P(tensor, None),
        P(context),
    )
    return jax.shard_map(
        per_device, mesh=fine, in_specs=in_specs, out_specs=P(context + tensor, None), check_vma=False
    )
```

```python
import functools

import jax
import jax.numpy as jnp
from jax import lax
from jax.experimental import pallas as pl
from jax.experimental.pallas import tpu as pltpu
from jax.sharding import Mesh
from jax.sharding import PartitionSpec as P

AXES = ("z_lo", "x", "z_hi", "y", "core")
SPAN = 128
RIM = 16


def swap(value, axis):
    return lax.ppermute(value, axis, [(0, 1), (1, 0)])


def shift(value, axis, by):
    size = lax.axis_size(axis)
    return lax.ppermute(value, axis, [(i, (i + by) % size) for i in range(size)])


def fan(axis):
    size = lax.axis_size(axis)
    return [(2 * i + c, 2 * ((i + 1 - 2 * c) % size) + c) for i in range(size) for c in range(2)]


def band_kernel(taps, band):
    groups, span = taps.shape
    for g in range(groups):
        row = jnp.concatenate([taps[g : g + 1, :], jnp.zeros((1, span), jnp.float32)], axis=1)
        rows = jnp.broadcast_to(row, (2 * span, 2 * span))
        moved = pltpu.roll(rows, 0, axis=1, stride=1, stride_axis=0)
        band[g] = moved[:, span:].astype(band.dtype)


def banded(long_filter):
    groups, span = long_filter.shape
    vmem = pl.BlockSpec(memory_space=pltpu.VMEM)
    return pl.pallas_call(
        band_kernel,
        out_shape=jax.ShapeDtypeStruct((groups, 2 * span, span), jnp.bfloat16),
        in_specs=[vmem],
        out_specs=vmem,
        compiler_params=pltpu.CompilerParams(vmem_limit_bytes=16 << 20),
        cost_estimate=pl.CostEstimate(flops=2_000_000_000, bytes_accessed=1_000_000, transcendentals=0),
    )(long_filter.astype(jnp.float32))


def across(value, by):
    size = lax.axis_size("z_lo")
    pairs = [(2 * i + h, 2 * ((i + by) % size) + 1 - h) for i in range(size) for h in range(2)]
    return lax.ppermute(value, ("z_lo", "z_hi"), pairs)


def ring(value, by):
    size = lax.axis_size("z_lo")
    pairs = []
    for i in range(size):
        for h in range(2):
            to = (h * size + i + by) % (2 * size)
            pairs.append((2 * i + h, 2 * (to % size) + to // size))
    return lax.ppermute(value, ("z_lo", "z_hi"), pairs)


def spread_columns(piece, ends):
    z_lo = lax.axis_index("z_lo")
    size = lax.axis_size("z_lo")
    top, bottom = z_lo == size - 1, z_lo == 0
    up = ring(jnp.where(top, ends[0], piece), 1)
    down = ring(jnp.where(bottom, ends[0], piece), -1)
    pairs = []
    for h in range(2):
        pairs += [(2 * 1 + h, 2 * 2 + h), (2 * 2 + h, 2 * 1 + h)]
        pairs += [(2 * 0 + h, 2 * 3 + 1 - h), (2 * 3 + h, 2 * 0 + 1 - h)]
    onward = jnp.where(jnp.logical_or(top, bottom), ends[1], jnp.where(z_lo == 1, up, down))
    opposite = lax.ppermute(onward, ("z_lo", "z_hi"), pairs)
    return piece, up, down, opposite


def spread_rows(mine):
    below, above = shift(mine, "x", 1), shift(mine, "x", -1)
    return below, above, jnp.where(lax.axis_index("core") == 0, below, above)


def places_of(by):
    z_lo, x = lax.axis_index("z_lo"), lax.axis_index("x")
    depth, size = lax.axis_size("z_lo"), lax.axis_size("x")
    first = (z_lo - by + depth) % depth * size
    return [first + x, first + (x + size - 1) % size, first + (x + 1) % size, first + (x + 2) % size]


def add_product_kernel(count, places, left, *refs):
    rights, rest = refs[:count], refs[count:]
    deep = rights[0].shape[0]
    step = 256
    for first in range(0, left.shape[0], step):
        rows = slice(first, first + step)
        total = rest[0][rows, :] if len(rest) == 2 else None
        for n, right in enumerate(rights):
            columns = pl.ds(pl.multiple_of(places[n] * deep, deep), deep)
            term = jnp.dot(left[rows, columns], right[...], preferred_element_type=jnp.float32)
            total = term if total is None else total + term
        rest[-1][rows, :] = total.astype(rest[-1].dtype)


def add_product(left, pieces, places, total, dtype):
    length = left.shape[0]
    deep, wide = pieces[0].shape
    count = len(pieces)
    vmem = pl.BlockSpec(memory_space=pltpu.VMEM)
    given = [left, *pieces] + ([] if total is None else [total])
    return pl.pallas_call(
        functools.partial(add_product_kernel, count),
        out_shape=jax.ShapeDtypeStruct((length, wide), dtype),
        in_specs=[pl.BlockSpec(memory_space=pltpu.SMEM)] + [vmem] * len(given),
        out_specs=vmem,
        compiler_params=pltpu.CompilerParams(vmem_limit_bytes=24 << 20),
        cost_estimate=pl.CostEstimate(
            flops=2 * length * deep * wide * count, bytes_accessed=8_000_000, transcendentals=0
        ),
    )(jnp.stack(places).astype(jnp.int32), *given)


def add_returned_kernel(half, tokens, returned, out):
    rows = tokens.shape[0]
    sources = returned.shape[0] // rows
    channels = returned.shape[1] // 2
    for side in range(2):
        for n in range(sources):
            first = ((half[0] if side == 0 else 1 - half[0]) * sources + n) * channels
            columns = pl.ds(pl.multiple_of(first, channels), channels)
            gated = returned[n * rows : (n + 1) * rows, side * channels : (side + 1) * channels]
            total = tokens[:, columns].astype(jnp.float32) + gated.astype(jnp.float32)
            out[:, columns] = total.astype(out.dtype)


def add_returned(tokens, returned, half):
    vmem = pl.BlockSpec(memory_space=pltpu.VMEM)
    return pl.pallas_call(
        add_returned_kernel,
        out_shape=jax.ShapeDtypeStruct(tokens.shape, jnp.bfloat16),
        in_specs=[pl.BlockSpec(memory_space=pltpu.SMEM), vmem, vmem],
        out_specs=vmem,
        compiler_params=pltpu.CompilerParams(vmem_limit_bytes=16 << 20),
        cost_estimate=pl.CostEstimate(flops=1_000_000, bytes_accessed=3_000_000, transcendentals=0),
    )(half[None].astype(jnp.int32), tokens, returned)


def mix_conv_kernel(
    flags, proj, halo, short, band, start_col, start_row, into, out, key_value_t, query, conv_t
):
    del into
    length, channels = out.shape
    groups = band.shape[0]
    share = channels // groups
    blocks = length // SPAN
    taps = short.shape[0] // 3
    key_value_t[:, 0:SPAN] = halo[0:SPAN, :].astype(jnp.float32).T.astype(jnp.bfloat16)
    for b in range(blocks):
        rows = slice(b * SPAN, (b + 1) * SPAN)
        starts = start_col[rows, :]
        places = b * SPAN + lax.broadcasted_iota(jnp.int32, (SPAN, 1), 0)
        mixed = []
        for m in range(3):
            cols = slice(m * channels, (m + 1) * channels)
            if b == 0:
                before = halo[SPAN + m * RIM : SPAN + (m + 1) * RIM, :]
            else:
                before = proj[b * SPAN - RIM : b * SPAN, cols]
            both = jnp.concatenate([before, proj[rows, cols]], axis=0).astype(jnp.float32)
            total = None
            for s in range(taps):
                term = short[m * taps + s : m * taps + s + 1, :] * both[RIM - s : RIM - s + SPAN]
                term = jnp.where(places - s >= starts, term, 0.0)
                total = term if total is None else total + term
            mixed.append(total)
        query[rows, :] = mixed[0]
        key_value_t[:, (b + 1) * SPAN : (b + 2) * SPAN] = (mixed[1] * mixed[2]).T.astype(jnp.bfloat16)
    for g in range(groups):
        rows = slice(g * share, (g + 1) * share)
        windows = jnp.concatenate(
            [key_value_t[rows, b * SPAN : (b + 2) * SPAN] for b in range(blocks)], axis=0
        )
        sums = jnp.dot(windows, band[g], preferred_element_type=jnp.float32)
        for b in range(blocks):
            conv_t[rows, b * SPAN : (b + 1) * SPAN] = sums[b * share : (b + 1) * share]
    for b in range(blocks):

        @pl.when(flags[b] > 0)
        def _(b=b):
            inputs = (b - 1) * SPAN + lax.broadcasted_iota(jnp.int32, (2 * SPAN, SPAN), 0)
            kept = (inputs >= start_row[:, b * SPAN : (b + 1) * SPAN])

            def one_group(g, _):
                rows = pl.ds(pl.multiple_of(g * share, share), share)
                weights = jnp.where(kept, band[g].astype(jnp.float32), 0.0).astype(jnp.bfloat16)
                conv_t[rows, b * SPAN : (b + 1) * SPAN] = jnp.dot(
                    key_value_t[rows, b * SPAN : (b + 2) * SPAN],
                    weights,
                    preferred_element_type=jnp.float32,
                )
                return 0

            lax.fori_loop(0, groups, one_group, 0, unroll=4)

    for b in range(blocks):
        rows = slice(b * SPAN, (b + 1) * SPAN)
        out[rows, :] = (query[rows, :] * conv_t[:, b * SPAN : (b + 1) * SPAN].T).astype(out.dtype)


def mix_conv(proj, halo, short, band, starts, rows, into, side):
    length, channels = proj.shape[0], proj.shape[1] // 3
    blocks = rows // SPAN
    starts = starts[:rows]
    last = starts.reshape(blocks, SPAN)[:, -1]
    flags = (last > jnp.arange(blocks, dtype=jnp.int32) * SPAN - (SPAN - 1)).astype(jnp.int32)
    given = [flags, proj, halo, short, band, starts[:, None], starts[None, :]]
    in_specs = [pl.BlockSpec(memory_space=pltpu.SMEM), pl.BlockSpec((rows, 3 * channels), lambda n: (0, 0))]
    in_specs += [pl.BlockSpec(memory_space=pltpu.VMEM)] * 5
    body = mix_conv_kernel
    aliases = {}
    if into is None:
        body = lambda *refs: mix_conv_kernel(*refs[:7], None, *refs[7:])
    else:
        aliases = {len(given): 0}
        given.append(into)
        in_specs.append(pl.BlockSpec(memory_space=pl.ANY))
    return pl.pallas_call(
        body,
        out_shape=jax.ShapeDtypeStruct((length, 2 * channels), jnp.bfloat16),
        grid=(1,),
        in_specs=in_specs,
        out_specs=pl.BlockSpec((rows, channels), lambda n: (0, side)),
        scratch_shapes=[
            pltpu.VMEM((channels, rows + SPAN), jnp.bfloat16),
            pltpu.VMEM((rows, channels), jnp.float32),
            pltpu.VMEM((channels, rows), jnp.float32),
        ],
        input_output_aliases=aliases,
        compiler_params=pltpu.CompilerParams(vmem_limit_bytes=24 << 20),
        cost_estimate=pl.CostEstimate(flops=rows * 6_000_000, bytes_accessed=4_000_000, transcendentals=0),
    )(*given)


def tail_of(proj, short, starts):
    length = proj.shape[0]
    channels = proj.shape[1] // 3
    taps = short.shape[0] // 3
    places = jnp.arange(length - SPAN, length, dtype=jnp.int32)
    mixed = []
    for m in (1, 2):
        total = jnp.zeros((SPAN, channels), jnp.float32)
        for s in range(taps):
            rows = proj[length - SPAN - s : length - s, m * channels : (m + 1) * channels].astype(jnp.float32)
            kept = (places - s >= starts[length - SPAN :])[:, None]
            total = total + jnp.where(kept, short[m * taps + s][None] * rows, 0.0)
        mixed.append(total)
    key_value = (mixed[0] * mixed[1]).astype(jnp.bfloat16)
    rims = [proj[length - RIM :, m * channels : (m + 1) * channels] for m in range(3)]
    return jnp.concatenate([key_value, *rims], axis=0)


def per_device(tokens, norm_gain, in_weight, short_filter, long_filter, doc_start):
    rows, width = tokens.shape
    channels = in_weight.shape[2]
    groups, span = long_filter.shape
    taps = short_filter.shape[1]
    z_lo, x, z_hi = lax.axis_index("z_lo"), lax.axis_index("x"), lax.axis_index("z_hi")
    contexts = lax.axis_size("z_lo") * lax.axis_size("x")
    context = z_lo * lax.axis_size("x") + x
    length = rows * lax.axis_size("y") * lax.axis_size("core")
    starts = lax.dynamic_slice_in_dim(doc_start, z_hi * length, length, 0)
    starts = starts - (context * lax.axis_size("z_hi") + z_hi) * length

    deep = width // contexts
    depth = lax.axis_size("z_lo")

    def cut(quarter):
        first = (quarter * lax.axis_size("x") + x) * deep
        return lax.dynamic_slice_in_dim(in_weight, first, deep, 0).reshape(deep, 3 * channels)

    piece, tokens = lax.optimization_barrier((cut((z_lo + 2) % depth), tokens))
    piece = across(piece, 2)
    top = z_lo == depth - 1

    float_tokens = tokens.astype(jnp.float32)
    scale_rows = lax.rsqrt(jnp.mean(float_tokens * float_tokens, axis=-1, keepdims=True) + 1e-06)
    normed = (float_tokens * scale_rows * norm_gain.astype(jnp.float32)[None]).astype(jnp.bfloat16)
    in_weight, normed = lax.optimization_barrier((in_weight, normed))
    gathered = lax.all_gather(normed, ("y", "core"), axis=0, tiled=True)
    weight_t = in_weight.transpose(1, 2, 0).reshape(3 * channels, width)
    piece, weight_t = lax.optimization_barrier((piece, weight_t))
    ends = cut(jnp.where(top, depth - 1, 0)), cut(jnp.where(top, depth - 2, 1))
    piece, *ends = lax.optimization_barrier((piece, *ends))
    columns = spread_columns(piece, ends)

    small = jnp.concatenate(
        [short_filter.reshape(3 * taps, channels), long_filter.reshape(-1, channels)], axis=0
    )
    small = swap(small, "z_hi")
    other_short, other_long = small[: 3 * taps], small[3 * taps :].reshape(groups, span)

    next_half = [(i, i + 1) for i in range(contexts * lax.axis_size("z_hi") - 1)]

    def halo_of(projected, short):
        return lax.ppermute(tail_of(projected, short, starts), ("z_lo", "x", "z_hi"), next_half)

    own_short = short_filter.reshape(3 * taps, channels).astype(jnp.float32)
    other_short = other_short.astype(jnp.float32)
    late, gathered = lax.optimization_barrier((columns[2:], gathered))
    columns = (*columns[:2], *late)
    own_projected = lax.dot_general(
        gathered, weight_t, (((1,), (1,)), ((), ())), preferred_element_type=jnp.float32
    ).astype(jnp.bfloat16)
    rows_of = [spread_rows(mine) for mine in columns]
    pieces, places = [], []
    half = 8
    for n, (by, mine, (below, above, onward)) in enumerate(zip((0, 1, -1, 2), columns, rows_of)):
        if n == 2:
            first_sum = add_product(gathered, pieces, places, None, jnp.float32)
        if n == 3:
            onward, own_projected = lax.optimization_barrier((onward, own_projected))
        pieces += [mine, below, above, lax.ppermute(onward, ("x", "core"), fan("x"))]
        places += places_of(by)
    other_halo = halo_of(own_projected, own_short)
    own_band, other_band = banded(long_filter), banded(other_long)
    nothing = jnp.zeros((SPAN + 3 * RIM, channels), jnp.bfloat16)
    gated = mix_conv(own_projected, nothing, own_short, own_band, starts, length, None, 0)
    first_sum, gated = lax.optimization_barrier((first_sum, gated))
    other_projected = add_product(gathered, pieces[half:], places[half:], first_sum, jnp.bfloat16)
    own_halo = halo_of(other_projected, other_short)
    gated = mix_conv(other_projected, other_halo, other_short, other_band, starts, length, gated, 1)
    gated = mix_conv(own_projected, own_halo, own_short, own_band, starts, 2 * SPAN, gated, 0)
    returned = lax.all_to_all(gated, ("y", "core"), split_axis=0, concat_axis=0, tiled=True)
    return add_returned(tokens, returned, z_hi)


def solution(mesh):
    fine = Mesh(mesh.devices.reshape(4, 4, 2, 4, 2), AXES)
    context, tensor = ("z_lo", "x"), ("z_hi", "y", "core")
    in_specs = (
        P(context + tensor, None),
        P(),
        P(None, None, tensor),
        P(None, None, tensor),
        P(tensor, None),
        P(context),
    )
    return jax.shard_map(
        per_device, mesh=fine, in_specs=in_specs, out_specs=P(context + tensor, None), check_vma=False
    )
```

```python
import functools

import jax
import jax.numpy as jnp
from jax import lax
from jax.experimental import pallas as pl
from jax.experimental.pallas import tpu as pltpu
from jax.sharding import Mesh
from jax.sharding import PartitionSpec as P

AXES = ("z_lo", "x", "z_hi", "y", "core")
SPAN = 128
RIM = 16


def swap(value, axis):
    return lax.ppermute(value, axis, [(0, 1), (1, 0)])


def shift(value, axis, by):
    size = lax.axis_size(axis)
    return lax.ppermute(value, axis, [(i, (i + by) % size) for i in range(size)])


def fan(axis):
    size = lax.axis_size(axis)
    return [(2 * i + c, 2 * ((i + 1 - 2 * c) % size) + c) for i in range(size) for c in range(2)]


def band_kernel(taps, band):
    groups, span = taps.shape
    for g in range(groups):
        row = jnp.concatenate([taps[g : g + 1, :], jnp.zeros((1, span), jnp.float32)], axis=1)
        rows = jnp.broadcast_to(row, (2 * span, 2 * span))
        moved = pltpu.roll(rows, 0, axis=1, stride=1, stride_axis=0)
        band[g] = moved[:, span:].astype(band.dtype)


def banded(long_filter):
    groups, span = long_filter.shape
    vmem = pl.BlockSpec(memory_space=pltpu.VMEM)
    return pl.pallas_call(
        band_kernel,
        out_shape=jax.ShapeDtypeStruct((groups, 2 * span, span), jnp.bfloat16),
        in_specs=[vmem],
        out_specs=vmem,
        compiler_params=pltpu.CompilerParams(vmem_limit_bytes=16 << 20),
        cost_estimate=pl.CostEstimate(flops=2_000_000_000, bytes_accessed=1_000_000, transcendentals=0),
    )(long_filter.astype(jnp.float32))


def across(value, by):
    size = lax.axis_size("z_lo")
    pairs = [(2 * i + h, 2 * ((i + by) % size) + 1 - h) for i in range(size) for h in range(2)]
    return lax.ppermute(value, ("z_lo", "z_hi"), pairs)


def ring(value, by):
    size = lax.axis_size("z_lo")
    pairs = []
    for i in range(size):
        for h in range(2):
            to = (h * size + i + by) % (2 * size)
            pairs.append((2 * i + h, 2 * (to % size) + to // size))
    return lax.ppermute(value, ("z_lo", "z_hi"), pairs)


def spread_columns(piece, ends):
    z_lo = lax.axis_index("z_lo")
    size = lax.axis_size("z_lo")
    top, bottom = z_lo == size - 1, z_lo == 0
    up = ring(jnp.where(top, ends[0], piece), 1)
    down = ring(jnp.where(bottom, ends[0], piece), -1)
    pairs = []
    for h in range(2):
        pairs += [(2 * 1 + h, 2 * 2 + h), (2 * 2 + h, 2 * 1 + h)]
        pairs += [(2 * 0 + h, 2 * 3 + 1 - h), (2 * 3 + h, 2 * 0 + 1 - h)]
    onward = jnp.where(jnp.logical_or(top, bottom), ends[1], jnp.where(z_lo == 1, up, down))
    opposite = lax.ppermute(onward, ("z_lo", "z_hi"), pairs)
    return (0, piece), (1, up), (-1, down), (2, opposite)


def spread_rows(mine):
    below, above = shift(mine, "x", 1), shift(mine, "x", -1)
    return below, above, jnp.where(lax.axis_index("core") == 0, below, above)


def places_of(by):
    z_lo, x = lax.axis_index("z_lo"), lax.axis_index("x")
    depth, size = lax.axis_size("z_lo"), lax.axis_size("x")
    first = (z_lo - by + depth) % depth * size
    return [first + x, first + (x + size - 1) % size, first + (x + 1) % size, first + (x + 2) % size]


def add_product_kernel(count, places, left, *refs):
    rights, rest = refs[:count], refs[count:]
    deep = rights[0].shape[0]
    step = 256
    for first in range(0, left.shape[0], step):
        rows = slice(first, first + step)
        total = rest[0][rows, :] if len(rest) == 2 else None
        for n, right in enumerate(rights):
            columns = pl.ds(pl.multiple_of(places[n] * deep, deep), deep)
            term = jnp.dot(left[rows, columns], right[...], preferred_element_type=jnp.float32)
            total = term if total is None else total + term
        rest[-1][rows, :] = total.astype(rest[-1].dtype)


def add_product(left, pieces, places, total, dtype):
    length = left.shape[0]
    deep, wide = pieces[0].shape
    count = len(pieces)
    vmem = pl.BlockSpec(memory_space=pltpu.VMEM)
    given = [left, *pieces] + ([] if total is None else [total])
    return pl.pallas_call(
        functools.partial(add_product_kernel, count),
        out_shape=jax.ShapeDtypeStruct((length, wide), dtype),
        in_specs=[pl.BlockSpec(memory_space=pltpu.SMEM)] + [vmem] * len(given),
        out_specs=vmem,
        compiler_params=pltpu.CompilerParams(vmem_limit_bytes=24 << 20),
        cost_estimate=pl.CostEstimate(
            flops=2 * length * deep * wide * count, bytes_accessed=8_000_000, transcendentals=0
        ),
    )(jnp.stack(places).astype(jnp.int32), *given)


def add_returned_kernel(half, tokens, returned, out):
    rows = tokens.shape[0]
    sources = returned.shape[0] // rows
    channels = returned.shape[1] // 2
    for side in range(2):
        for n in range(sources):
            first = ((half[0] if side == 0 else 1 - half[0]) * sources + n) * channels
            columns = pl.ds(pl.multiple_of(first, channels), channels)
            gated = returned[n * rows : (n + 1) * rows, side * channels : (side + 1) * channels]
            total = tokens[:, columns].astype(jnp.float32) + gated.astype(jnp.float32)
            out[:, columns] = total.astype(out.dtype)


def add_returned(tokens, returned, half):
    vmem = pl.BlockSpec(memory_space=pltpu.VMEM)
    return pl.pallas_call(
        add_returned_kernel,
        out_shape=jax.ShapeDtypeStruct(tokens.shape, jnp.bfloat16),
        in_specs=[pl.BlockSpec(memory_space=pltpu.SMEM), vmem, vmem],
        out_specs=vmem,
        compiler_params=pltpu.CompilerParams(vmem_limit_bytes=16 << 20),
        cost_estimate=pl.CostEstimate(flops=1_000_000, bytes_accessed=3_000_000, transcendentals=0),
    )(half[None].astype(jnp.int32), tokens, returned)


def mix_conv_kernel(
    flags, proj, halo, short, band, start_col, start_row, into, out, key_value_t, query, conv_t
):
    del into
    length, channels = out.shape
    groups = band.shape[0]
    share = channels // groups
    blocks = length // SPAN
    taps = short.shape[0] // 3
    key_value_t[:, 0:SPAN] = halo[0:SPAN, :].astype(jnp.float32).T.astype(jnp.bfloat16)
    for b in range(blocks):
        rows = slice(b * SPAN, (b + 1) * SPAN)
        starts = start_col[rows, :]
        places = b * SPAN + lax.broadcasted_iota(jnp.int32, (SPAN, 1), 0)
        mixed = []
        for m in range(3):
            cols = slice(m * channels, (m + 1) * channels)
            if b == 0:
                before = halo[SPAN + m * RIM : SPAN + (m + 1) * RIM, :]
            else:
                before = proj[b * SPAN - RIM : b * SPAN, cols]
            both = jnp.concatenate([before, proj[rows, cols]], axis=0).astype(jnp.float32)
            total = None
            for s in range(taps):
                term = short[m * taps + s : m * taps + s + 1, :] * both[RIM - s : RIM - s + SPAN]
                term = jnp.where(places - s >= starts, term, 0.0)
                total = term if total is None else total + term
            mixed.append(total)
        query[rows, :] = mixed[0]
        key_value_t[:, (b + 1) * SPAN : (b + 2) * SPAN] = (mixed[1] * mixed[2]).T.astype(jnp.bfloat16)
    for g in range(groups):
        rows = slice(g * share, (g + 1) * share)
        windows = jnp.concatenate(
            [key_value_t[rows, b * SPAN : (b + 2) * SPAN] for b in range(blocks)], axis=0
        )
        sums = jnp.dot(windows, band[g], preferred_element_type=jnp.float32)
        for b in range(blocks):
            conv_t[rows, b * SPAN : (b + 1) * SPAN] = sums[b * share : (b + 1) * share]
    for b in range(blocks):

        @pl.when(flags[b] > 0)
        def _(b=b):
            inputs = (b - 1) * SPAN + lax.broadcasted_iota(jnp.int32, (2 * SPAN, SPAN), 0)
            kept = (inputs >= start_row[:, b * SPAN : (b + 1) * SPAN])

            def one_group(g, _):
                rows = pl.ds(pl.multiple_of(g * share, share), share)
                weights = jnp.where(kept, band[g].astype(jnp.float32), 0.0).astype(jnp.bfloat16)
                conv_t[rows, b * SPAN : (b + 1) * SPAN] = jnp.dot(
                    key_value_t[rows, b * SPAN : (b + 2) * SPAN],
                    weights,
                    preferred_element_type=jnp.float32,
                )
                return 0

            lax.fori_loop(0, groups, one_group, 0, unroll=4)

    for b in range(blocks):
        rows = slice(b * SPAN, (b + 1) * SPAN)
        out[rows, :] = (query[rows, :] * conv_t[:, b * SPAN : (b + 1) * SPAN].T).astype(out.dtype)


def mix_conv(proj, halo, short, band, starts, rows, into, side):
    length, channels = proj.shape[0], proj.shape[1] // 3
    blocks = rows // SPAN
    starts = starts[:rows]
    last = starts.reshape(blocks, SPAN)[:, -1]
    flags = (last > jnp.arange(blocks, dtype=jnp.int32) * SPAN - (SPAN - 1)).astype(jnp.int32)
    given = [flags, proj, halo, short, band, starts[:, None], starts[None, :]]
    in_specs = [pl.BlockSpec(memory_space=pltpu.SMEM), pl.BlockSpec((rows, 3 * channels), lambda n: (0, 0))]
    in_specs += [pl.BlockSpec(memory_space=pltpu.VMEM)] * 5
    body = mix_conv_kernel
    aliases = {}
    if into is None:
        body = lambda *refs: mix_conv_kernel(*refs[:7], None, *refs[7:])
    else:
        aliases = {len(given): 0}
        given.append(into)
        in_specs.append(pl.BlockSpec(memory_space=pl.ANY))
    return pl.pallas_call(
        body,
        out_shape=jax.ShapeDtypeStruct((length, 2 * channels), jnp.bfloat16),
        grid=(1,),
        in_specs=in_specs,
        out_specs=pl.BlockSpec((rows, channels), lambda n: (0, side)),
        scratch_shapes=[
            pltpu.VMEM((channels, rows + SPAN), jnp.bfloat16),
            pltpu.VMEM((rows, channels), jnp.float32),
            pltpu.VMEM((channels, rows), jnp.float32),
        ],
        input_output_aliases=aliases,
        compiler_params=pltpu.CompilerParams(vmem_limit_bytes=24 << 20),
        cost_estimate=pl.CostEstimate(flops=rows * 6_000_000, bytes_accessed=4_000_000, transcendentals=0),
    )(*given)


def tail_of(proj, short, starts):
    length = proj.shape[0]
    channels = proj.shape[1] // 3
    taps = short.shape[0] // 3
    places = jnp.arange(length - SPAN, length, dtype=jnp.int32)
    mixed = []
    for m in (1, 2):
        total = jnp.zeros((SPAN, channels), jnp.float32)
        for s in range(taps):
            rows = proj[length - SPAN - s : length - s, m * channels : (m + 1) * channels].astype(jnp.float32)
            kept = (places - s >= starts[length - SPAN :])[:, None]
            total = total + jnp.where(kept, short[m * taps + s][None] * rows, 0.0)
        mixed.append(total)
    key_value = (mixed[0] * mixed[1]).astype(jnp.bfloat16)
    rims = [proj[length - RIM :, m * channels : (m + 1) * channels] for m in range(3)]
    return jnp.concatenate([key_value, *rims], axis=0)


def per_device(tokens, norm_gain, in_weight, short_filter, long_filter, doc_start):
    rows, width = tokens.shape
    channels = in_weight.shape[2]
    groups, span = long_filter.shape
    taps = short_filter.shape[1]
    z_lo, x, z_hi = lax.axis_index("z_lo"), lax.axis_index("x"), lax.axis_index("z_hi")
    contexts = lax.axis_size("z_lo") * lax.axis_size("x")
    context = z_lo * lax.axis_size("x") + x
    length = rows * lax.axis_size("y") * lax.axis_size("core")
    starts = lax.dynamic_slice_in_dim(doc_start, z_hi * length, length, 0)
    starts = starts - (context * lax.axis_size("z_hi") + z_hi) * length

    deep = width // contexts
    depth = lax.axis_size("z_lo")

    def cut(quarter):
        first = (quarter * lax.axis_size("x") + x) * deep
        return lax.dynamic_slice_in_dim(in_weight, first, deep, 0).reshape(deep, 3 * channels)

    piece, tokens = lax.optimization_barrier((cut((z_lo + 2) % depth), tokens))
    piece = across(piece, 2)
    top = z_lo == depth - 1

    float_tokens = tokens.astype(jnp.float32)
    scale_rows = lax.rsqrt(jnp.mean(float_tokens * float_tokens, axis=-1, keepdims=True) + 1e-06)
    normed = (float_tokens * scale_rows * norm_gain.astype(jnp.float32)[None]).astype(jnp.bfloat16)
    in_weight, normed = lax.optimization_barrier((in_weight, normed))
    gathered = lax.all_gather(normed, ("y", "core"), axis=0, tiled=True)
    weight_t = in_weight.transpose(1, 2, 0).reshape(3 * channels, width)
    piece, weight_t = lax.optimization_barrier((piece, weight_t))
    ends = cut(jnp.where(top, depth - 1, 0)), cut(jnp.where(top, depth - 2, 1))
    piece, *ends = lax.optimization_barrier((piece, *ends))
    columns = spread_columns(piece, ends)

    small = jnp.concatenate(
        [short_filter.reshape(3 * taps, channels), long_filter.reshape(-1, channels)], axis=0
    )
    small = swap(small, "z_hi")
    other_short, other_long = small[: 3 * taps], small[3 * taps :].reshape(groups, span)

    next_half = [(i, i + 1) for i in range(contexts * lax.axis_size("z_hi") - 1)]

    def halo_of(projected, short):
        return lax.ppermute(tail_of(projected, short, starts), ("z_lo", "x", "z_hi"), next_half)

    own_short = short_filter.reshape(3 * taps, channels).astype(jnp.float32)
    other_short = other_short.astype(jnp.float32)
    own_projected = lax.dot_general(
        gathered, weight_t, (((1,), (1,)), ((), ())), preferred_element_type=jnp.float32
    ).astype(jnp.bfloat16)
    (_, mine) = columns[3]
    mine, own_projected = lax.optimization_barrier((mine, own_projected))
    columns = (*columns[:3], (columns[3][0], mine))
    rows_of = [spread_rows(mine) for _, mine in columns]
    pieces, places = [], []
    other_halo = halo_of(own_projected, own_short)
    half = 8
    for n, ((by, mine), (below, above, onward)) in enumerate(zip(columns, rows_of)):
        if n == 2:
            pieces[0], other_halo = lax.optimization_barrier((pieces[0], other_halo))
            first_sum = add_product(gathered, pieces, places, None, jnp.float32)
        if n == 3:
            onward, first_sum = lax.optimization_barrier((onward, first_sum))
        pieces += [mine, below, above, lax.ppermute(onward, ("x", "core"), fan("x"))]
        places += places_of(by)
    own_band, other_band = banded(long_filter), banded(other_long)
    nothing = jnp.zeros((SPAN + 3 * RIM, channels), jnp.bfloat16)
    gated = mix_conv(own_projected, nothing, own_short, own_band, starts, length, None, 0)
    first_sum, gated = lax.optimization_barrier((first_sum, gated))
    other_projected = add_product(gathered, pieces[half:], places[half:], first_sum, jnp.bfloat16)
    own_halo = halo_of(other_projected, other_short)
    gated = mix_conv(other_projected, other_halo, other_short, other_band, starts, length, gated, 1)
    gated = mix_conv(own_projected, own_halo, own_short, own_band, starts, 2 * SPAN, gated, 0)
    returned = lax.all_to_all(gated, ("y", "core"), split_axis=0, concat_axis=0, tiled=True)
    return add_returned(tokens, returned, z_hi)


def solution(mesh):
    fine = Mesh(mesh.devices.reshape(4, 4, 2, 4, 2), AXES)
    context, tensor = ("z_lo", "x"), ("z_hi", "y", "core")
    in_specs = (
        P(context + tensor, None),
        P(),
        P(None, None, tensor),
        P(None, None, tensor),
        P(tensor, None),
        P(context),
    )
    return jax.shard_map(
        per_device, mesh=fine, in_specs=in_specs, out_specs=P(context + tensor, None), check_vma=False
    )
```

```python
import functools

import jax
import jax.numpy as jnp
from jax import lax
from jax.experimental import pallas as pl
from jax.experimental.pallas import tpu as pltpu
from jax.sharding import Mesh
from jax.sharding import PartitionSpec as P

AXES = ("z_lo", "x", "z_hi", "y", "core")
SPAN = 128
RIM = 16


def swap(value, axis):
    return lax.ppermute(value, axis, [(0, 1), (1, 0)])


def shift(value, axis, by):
    size = lax.axis_size(axis)
    return lax.ppermute(value, axis, [(i, (i + by) % size) for i in range(size)])


def fan(axis):
    size = lax.axis_size(axis)
    return [(2 * i + c, 2 * ((i + 1 - 2 * c) % size) + c) for i in range(size) for c in range(2)]


def band_kernel(taps, band):
    groups, span = taps.shape
    for g in range(groups):
        row = jnp.concatenate([taps[g : g + 1, :], jnp.zeros((1, span), jnp.float32)], axis=1)
        rows = jnp.broadcast_to(row, (2 * span, 2 * span))
        moved = pltpu.roll(rows, 0, axis=1, stride=1, stride_axis=0)
        band[g] = moved[:, span:].astype(band.dtype)


def banded(long_filter):
    groups, span = long_filter.shape
    vmem = pl.BlockSpec(memory_space=pltpu.VMEM)
    return pl.pallas_call(
        band_kernel,
        out_shape=jax.ShapeDtypeStruct((groups, 2 * span, span), jnp.bfloat16),
        in_specs=[vmem],
        out_specs=vmem,
        compiler_params=pltpu.CompilerParams(vmem_limit_bytes=16 << 20),
        cost_estimate=pl.CostEstimate(flops=2_000_000_000, bytes_accessed=1_000_000, transcendentals=0),
    )(long_filter.astype(jnp.float32))


def across(value, by):
    size = lax.axis_size("z_lo")
    pairs = [(2 * i + h, 2 * ((i + by) % size) + 1 - h) for i in range(size) for h in range(2)]
    return lax.ppermute(value, ("z_lo", "z_hi"), pairs)


def ring(value, by):
    size = lax.axis_size("z_lo")
    pairs = []
    for i in range(size):
        for h in range(2):
            to = (h * size + i + by) % (2 * size)
            pairs.append((2 * i + h, 2 * (to % size) + to // size))
    return lax.ppermute(value, ("z_lo", "z_hi"), pairs)


def spread_columns(piece, ends):
    z_lo = lax.axis_index("z_lo")
    size = lax.axis_size("z_lo")
    top, bottom = z_lo == size - 1, z_lo == 0
    up = ring(jnp.where(top, ends[0], piece), 1)
    down = ring(jnp.where(bottom, ends[0], piece), -1)
    pairs = []
    for h in range(2):
        pairs += [(2 * 1 + h, 2 * 2 + h), (2 * 2 + h, 2 * 1 + h)]
        pairs += [(2 * 0 + h, 2 * 3 + 1 - h), (2 * 3 + h, 2 * 0 + 1 - h)]
    onward = jnp.where(jnp.logical_or(top, bottom), ends[1], jnp.where(z_lo == 1, up, down))
    opposite = lax.ppermute(onward, ("z_lo", "z_hi"), pairs)
    return (0, piece), (1, up), (-1, down), (2, opposite)


def spread_rows(mine):
    below, above = shift(mine, "x", 1), shift(mine, "x", -1)
    return below, above, jnp.where(lax.axis_index("core") == 0, below, above)


def places_of(by):
    z_lo, x = lax.axis_index("z_lo"), lax.axis_index("x")
    depth, size = lax.axis_size("z_lo"), lax.axis_size("x")
    first = (z_lo - by + depth) % depth * size
    return [first + x, first + (x + size - 1) % size, first + (x + 1) % size, first + (x + 2) % size]


def add_product_kernel(count, places, left, *refs):
    rights, rest = refs[:count], refs[count:]
    deep = rights[0].shape[0]
    step = 256
    for first in range(0, left.shape[0], step):
        rows = slice(first, first + step)
        total = rest[0][rows, :] if len(rest) == 2 else None
        for n, right in enumerate(rights):
            columns = pl.ds(pl.multiple_of(places[n] * deep, deep), deep)
            term = jnp.dot(left[rows, columns], right[...], preferred_element_type=jnp.float32)
            total = term if total is None else total + term
        rest[-1][rows, :] = total.astype(rest[-1].dtype)


def add_product(left, pieces, places, total, dtype):
    length = left.shape[0]
    deep, wide = pieces[0].shape
    count = len(pieces)
    vmem = pl.BlockSpec(memory_space=pltpu.VMEM)
    given = [left, *pieces] + ([] if total is None else [total])
    return pl.pallas_call(
        functools.partial(add_product_kernel, count),
        out_shape=jax.ShapeDtypeStruct((length, wide), dtype),
        in_specs=[pl.BlockSpec(memory_space=pltpu.SMEM)] + [vmem] * len(given),
        out_specs=vmem,
        compiler_params=pltpu.CompilerParams(vmem_limit_bytes=24 << 20),
        cost_estimate=pl.CostEstimate(
            flops=2 * length * deep * wide * count, bytes_accessed=8_000_000, transcendentals=0
        ),
    )(jnp.stack(places).astype(jnp.int32), *given)


def add_returned_kernel(half, tokens, returned, out):
    rows = tokens.shape[0]
    sources = returned.shape[0] // rows
    channels = returned.shape[1] // 2
    for side in range(2):
        for n in range(sources):
            first = ((half[0] if side == 0 else 1 - half[0]) * sources + n) * channels
            columns = pl.ds(pl.multiple_of(first, channels), channels)
            gated = returned[n * rows : (n + 1) * rows, side * channels : (side + 1) * channels]
            total = tokens[:, columns].astype(jnp.float32) + gated.astype(jnp.float32)
            out[:, columns] = total.astype(out.dtype)


def add_returned(tokens, returned, half):
    vmem = pl.BlockSpec(memory_space=pltpu.VMEM)
    return pl.pallas_call(
        add_returned_kernel,
        out_shape=jax.ShapeDtypeStruct(tokens.shape, jnp.bfloat16),
        in_specs=[pl.BlockSpec(memory_space=pltpu.SMEM), vmem, vmem],
        out_specs=vmem,
        compiler_params=pltpu.CompilerParams(vmem_limit_bytes=16 << 20),
        cost_estimate=pl.CostEstimate(flops=1_000_000, bytes_accessed=3_000_000, transcendentals=0),
    )(half[None].astype(jnp.int32), tokens, returned)


def mix_conv_kernel(
    flags, proj, halo, short, band, start_col, start_row, into, out, key_value_t, query, conv_t
):
    del into
    length, channels = out.shape
    groups = band.shape[0]
    share = channels // groups
    blocks = length // SPAN
    taps = short.shape[0] // 3
    key_value_t[:, 0:SPAN] = halo[0:SPAN, :].astype(jnp.float32).T.astype(jnp.bfloat16)
    for b in range(blocks):
        rows = slice(b * SPAN, (b + 1) * SPAN)
        starts = start_col[rows, :]
        places = b * SPAN + lax.broadcasted_iota(jnp.int32, (SPAN, 1), 0)
        mixed = []
        for m in range(3):
            cols = slice(m * channels, (m + 1) * channels)
            if b == 0:
                before = halo[SPAN + m * RIM : SPAN + (m + 1) * RIM, :]
            else:
                before = proj[b * SPAN - RIM : b * SPAN, cols]
            both = jnp.concatenate([before, proj[rows, cols]], axis=0).astype(jnp.float32)
            total = None
            for s in range(taps):
                term = short[m * taps + s : m * taps + s + 1, :] * both[RIM - s : RIM - s + SPAN]
                term = jnp.where(places - s >= starts, term, 0.0)
                total = term if total is None else total + term
            mixed.append(total)
        query[rows, :] = mixed[0]
        key_value_t[:, (b + 1) * SPAN : (b + 2) * SPAN] = (mixed[1] * mixed[2]).T.astype(jnp.bfloat16)
    for g in range(groups):
        rows = slice(g * share, (g + 1) * share)
        windows = jnp.concatenate(
            [key_value_t[rows, b * SPAN : (b + 2) * SPAN] for b in range(blocks)], axis=0
        )
        sums = jnp.dot(windows, band[g], preferred_element_type=jnp.float32)
        for b in range(blocks):
            conv_t[rows, b * SPAN : (b + 1) * SPAN] = sums[b * share : (b + 1) * share]
    for b in range(blocks):

        @pl.when(flags[b] > 0)
        def _(b=b):
            inputs = (b - 1) * SPAN + lax.broadcasted_iota(jnp.int32, (2 * SPAN, SPAN), 0)
            kept = (inputs >= start_row[:, b * SPAN : (b + 1) * SPAN])

            def one_group(g, _):
                rows = pl.ds(pl.multiple_of(g * share, share), share)
                weights = jnp.where(kept, band[g].astype(jnp.float32), 0.0).astype(jnp.bfloat16)
                conv_t[rows, b * SPAN : (b + 1) * SPAN] = jnp.dot(
                    key_value_t[rows, b * SPAN : (b + 2) * SPAN],
                    weights,
                    preferred_element_type=jnp.float32,
                )
                return 0

            lax.fori_loop(0, groups, one_group, 0, unroll=4)

    for b in range(blocks):
        rows = slice(b * SPAN, (b + 1) * SPAN)
        out[rows, :] = (query[rows, :] * conv_t[:, b * SPAN : (b + 1) * SPAN].T).astype(out.dtype)


def mix_conv(proj, halo, short, band, starts, rows, into, side):
    length, channels = proj.shape[0], proj.shape[1] // 3
    blocks = rows // SPAN
    starts = starts[:rows]
    last = starts.reshape(blocks, SPAN)[:, -1]
    flags = (last > jnp.arange(blocks, dtype=jnp.int32) * SPAN - (SPAN - 1)).astype(jnp.int32)
    given = [flags, proj, halo, short, band, starts[:, None], starts[None, :]]
    in_specs = [pl.BlockSpec(memory_space=pltpu.SMEM), pl.BlockSpec((rows, 3 * channels), lambda n: (0, 0))]
    in_specs += [pl.BlockSpec(memory_space=pltpu.VMEM)] * 5
    body = mix_conv_kernel
    aliases = {}
    if into is None:
        body = lambda *refs: mix_conv_kernel(*refs[:7], None, *refs[7:])
    else:
        aliases = {len(given): 0}
        given.append(into)
        in_specs.append(pl.BlockSpec(memory_space=pl.ANY))
    return pl.pallas_call(
        body,
        out_shape=jax.ShapeDtypeStruct((length, 2 * channels), jnp.bfloat16),
        grid=(1,),
        in_specs=in_specs,
        out_specs=pl.BlockSpec((rows, channels), lambda n: (0, side)),
        scratch_shapes=[
            pltpu.VMEM((channels, rows + SPAN), jnp.bfloat16),
            pltpu.VMEM((rows, channels), jnp.float32),
            pltpu.VMEM((channels, rows), jnp.float32),
        ],
        input_output_aliases=aliases,
        compiler_params=pltpu.CompilerParams(vmem_limit_bytes=24 << 20),
        cost_estimate=pl.CostEstimate(flops=rows * 6_000_000, bytes_accessed=4_000_000, transcendentals=0),
    )(*given)


def tail_of(proj, short, starts):
    length = proj.shape[0]
    channels = proj.shape[1] // 3
    taps = short.shape[0] // 3
    places = jnp.arange(length - SPAN, length, dtype=jnp.int32)
    mixed = []
    for m in (1, 2):
        total = jnp.zeros((SPAN, channels), jnp.float32)
        for s in range(taps):
            rows = proj[length - SPAN - s : length - s, m * channels : (m + 1) * channels].astype(jnp.float32)
            kept = (places - s >= starts[length - SPAN :])[:, None]
            total = total + jnp.where(kept, short[m * taps + s][None] * rows, 0.0)
        mixed.append(total)
    key_value = (mixed[0] * mixed[1]).astype(jnp.bfloat16)
    rims = [proj[length - RIM :, m * channels : (m + 1) * channels] for m in range(3)]
    return jnp.concatenate([key_value, *rims], axis=0)


def per_device(tokens, norm_gain, in_weight, short_filter, long_filter, doc_start):
    rows, width = tokens.shape
    channels = in_weight.shape[2]
    groups, span = long_filter.shape
    taps = short_filter.shape[1]
    z_lo, x, z_hi = lax.axis_index("z_lo"), lax.axis_index("x"), lax.axis_index("z_hi")
    contexts = lax.axis_size("z_lo") * lax.axis_size("x")
    context = z_lo * lax.axis_size("x") + x
    length = rows * lax.axis_size("y") * lax.axis_size("core")
    starts = lax.dynamic_slice_in_dim(doc_start, z_hi * length, length, 0)
    starts = starts - (context * lax.axis_size("z_hi") + z_hi) * length

    deep = width // contexts
    depth = lax.axis_size("z_lo")

    def cut(quarter):
        first = (quarter * lax.axis_size("x") + x) * deep
        return lax.dynamic_slice_in_dim(in_weight, first, deep, 0).reshape(deep, 3 * channels)

    piece, tokens = lax.optimization_barrier((cut((z_lo + 2) % depth), tokens))
    piece = across(piece, 2)
    top = z_lo == depth - 1

    float_tokens = tokens.astype(jnp.float32)
    scale_rows = lax.rsqrt(jnp.mean(float_tokens * float_tokens, axis=-1, keepdims=True) + 1e-06)
    normed = (float_tokens * scale_rows * norm_gain.astype(jnp.float32)[None]).astype(jnp.bfloat16)
    in_weight, normed = lax.optimization_barrier((in_weight, normed))
    gathered = lax.all_gather(normed, ("y", "core"), axis=0, tiled=True)
    weight_t = in_weight.transpose(1, 2, 0).reshape(3 * channels, width)
    piece, weight_t = lax.optimization_barrier((piece, weight_t))
    ends = cut(jnp.where(top, depth - 1, 0)), cut(jnp.where(top, depth - 2, 1))
    piece, *ends = lax.optimization_barrier((piece, *ends))
    columns = spread_columns(piece, ends)

    small = jnp.concatenate(
        [short_filter.reshape(3 * taps, channels), long_filter.reshape(-1, channels)], axis=0
    )
    small = swap(small, "z_hi")
    other_short, other_long = small[: 3 * taps], small[3 * taps :].reshape(groups, span)

    next_half = [(i, i + 1) for i in range(contexts * lax.axis_size("z_hi") - 1)]

    own_short = short_filter.reshape(3 * taps, channels).astype(jnp.float32)
    other_short = other_short.astype(jnp.float32)
    own_projected = lax.dot_general(
        gathered, weight_t, (((1,), (1,)), ((), ())), preferred_element_type=jnp.float32
    ).astype(jnp.bfloat16)
    (_, mine) = columns[3]
    mine, own_projected = lax.optimization_barrier((mine, own_projected))
    columns = (*columns[:3], (columns[3][0], mine))
    rows_of = [spread_rows(mine) for _, mine in columns]
    pieces, places = [], []
    half = 8
    for n, ((by, mine), (below, above, onward)) in enumerate(zip(columns, rows_of)):
        if n == 2:
            first_sum = add_product(gathered, pieces, places, None, jnp.float32)
        if n == 3:
            onward, first_sum = lax.optimization_barrier((onward, first_sum))
        pieces += [mine, below, above, lax.ppermute(onward, ("x", "core"), fan("x"))]
        places += places_of(by)
    own_band, other_band = banded(long_filter), banded(other_long)
    nothing = jnp.zeros((SPAN + 3 * RIM, channels), jnp.bfloat16)
    gated = mix_conv(own_projected, nothing, own_short, own_band, starts, length, None, 0)
    first_sum, gated = lax.optimization_barrier((first_sum, gated))
    other_projected = add_product(gathered, pieces[half:], places[half:], first_sum, jnp.bfloat16)
    tails = jnp.concatenate(
        [tail_of(other_projected, other_short, starts), tail_of(own_projected, own_short, starts)], axis=0
    )
    halos = lax.ppermute(tails, ("z_lo", "x", "z_hi"), next_half)
    own_halo, other_halo = halos[: SPAN + 3 * RIM], halos[SPAN + 3 * RIM :]
    gated = mix_conv(other_projected, other_halo, other_short, other_band, starts, length, gated, 1)
    gated = mix_conv(own_projected, own_halo, own_short, own_band, starts, 2 * SPAN, gated, 0)
    returned = lax.all_to_all(gated, ("y", "core"), split_axis=0, concat_axis=0, tiled=True)
    return add_returned(tokens, returned, z_hi)


def solution(mesh):
    fine = Mesh(mesh.devices.reshape(4, 4, 2, 4, 2), AXES)
    context, tensor = ("z_lo", "x"), ("z_hi", "y", "core")
    in_specs = (
        P(context + tensor, None),
        P(),
        P(None, None, tensor),
        P(None, None, tensor),
        P(tensor, None),
        P(context),
    )
    return jax.shard_map(
        per_device, mesh=fine, in_specs=in_specs, out_specs=P(context + tensor, None), check_vma=False
    )
```
